32 devices in a mesh: seq: 4 (over y, x), pair: 8 (over z, core).
Axes of the slice: x: 2, y: 2, z: 4, core: 2. Of those that a mesh axis runs over, the one named last changes fastest.
Arguments:
- prompt_keys: bfloat16 [8, 1024, 512], P('pair', 'seq'), may hold values from -6 to 6
- prompt_values: bfloat16 [8, 1024, 512], P('pair', 'seq'), may hold values from -6 to 6
- resp_queries: bfloat16 [8, 2, 512, 2048], P('pair', None, 'seq'), may hold values from -26 to 26
- resp_keys: bfloat16 [8, 2, 512, 512], P('pair', None, 'seq'), may hold values from -6 to 6
- resp_values: bfloat16 [8, 2, 512, 512], P('pair', None, 'seq'), may hold values from -6 to 6
- seq_grad: bfloat16 [8, 2, 512, 2048], P('pair', None, 'seq'), may hold values from -48 to 48
- token_logratio: float32 [8, 2, 512], P('pair', None, 'seq'), may hold values from -0.35 to 0.35
- resp_len: int32 [8, 2], P('pair'), may hold values from 128 to 512, as said below
- prefer: int32 [8], replicated, may hold values from 0 to 1
Outputs:
- prompt_dk: float32 [8, 1024, 512], P('pair', 'seq')
- prompt_dv: float32 [8, 1024, 512], P('pair', 'seq')
- resp_dq: float32 [8, 2, 512, 2048], P('pair', None, 'seq')
- resp_dk: float32 [8, 2, 512, 512], P('pair', None, 'seq')
- resp_dv: float32 [8, 2, 512, 512], P('pair', None, 'seq')
- losses: float32 [8], P('pair')
The draws below stay inside these ranges and needn't reach their ends.
Inputs may be any that keep to these rules, and one draw needn't show every extreme that they name: `resp_len`: whole blocks of 128 tokens.
All inputs are finite; a program needn't handle non-finite values.
Results may differ from the reference program's by a relative error of at most 0.0074.
Values may be sent and summed in bfloat16 or wider, within the bound.
No kernel may reach another device: no remote copies, remote signals or barrier semaphores. Data moves between devices by JAX's collectives and lax.ppermute only.
A program may use at most 192 MiB of HBM per device.

```python
import math
import jax
import jax.numpy as jnp
from jax import lax

HEAD_DIM = 128
QUERY_HEADS = 16
KV_HEADS = 4
BLOCK_LEN = 128
PROMPT_LEN = 1024
RESP_LEN = 512
PROMPTS = 8


def draw_prompt_keys(key, part):
    key = jax.random.fold_in(key, 1)
    shape_all = (PROMPTS, PROMPT_LEN, KV_HEADS * HEAD_DIM)
    sampled = jnp.clip(jax.random.normal(key, shape_all), -6.0, 6.0)
    return sampled.astype(jnp.bfloat16)


def draw_resp_queries(key, part):
    key = jax.random.fold_in(key, 2)
    shape_all = (PROMPTS, 2, RESP_LEN, QUERY_HEADS * HEAD_DIM)
    sampled = 1.5 * jnp.clip(jax.random.normal(key, shape_all), -6.0, 6.0)
    return sampled.astype(jnp.bfloat16)


def draw_token_logratio(key, part):
    key = jax.random.fold_in(key, 3)
    places = jnp.arange(RESP_LEN, dtype=jnp.float32) / RESP_LEN
    offsets = jax.random.uniform(jax.random.fold_in(key, 1), (PROMPTS, 2, 1), minval=-0.002, maxval=0.002)
    growth = 1.0 + 2.0 * places
    jitter = 0.02 * jnp.clip(jax.random.normal(key, (PROMPTS, 2, RESP_LEN)), -4.0, 4.0)
    return (growth * (offsets + jitter)).astype(jnp.float32)


def draw_resp_len(key, part):
    key = jax.random.fold_in(key, 4)
    blocks = jax.random.randint(key, (PROMPTS * 2,), 1, RESP_LEN // BLOCK_LEN + 1)
    shuffled = jax.random.permutation(jax.random.fold_in(key, 1), PROMPTS * 2)
    blocks = blocks.at[shuffled[0]].set(RESP_LEN // BLOCK_LEN)
    blocks = blocks.at[shuffled[1]].set(1)
    return (blocks * BLOCK_LEN).reshape(PROMPTS, 2).astype(jnp.int32)


def set_ends(entries, rng, smallest, high):
    place = [jax.random.randint(jax.random.fold_in(rng, axis), (), 0, length) for axis, length in enumerate(entries.shape)]
    widest = entries.shape.index(max(entries.shape))
    next_to = place[:widest] + [(place[widest] + 1) % entries.shape[widest]] + place[widest + 1:]
    return entries.at[tuple(place)].set(smallest).at[tuple(next_to)].set(high)


def block_levels(rng, shape, cuts, least, high):
    def one(position, parts):
        draws = jax.random.uniform(jax.random.fold_in(jax.random.fold_in(rng, 6), position), (parts,), jnp.float32, least / len(cuts), high / len(cuts))
        return jnp.repeat(jnp.exp(draws), shape[position] // parts).reshape((-1,) + (1,) * (len(shape) - position - 1))

    loudness = one(*cuts[0])
    for cut in cuts[1:]:
        loudness = loudness * one(*cut)
    return loudness


def centred(key, dims, width, bound, shards=(), held_as=jnp.bfloat16):
    array = width * jax.random.normal(key, dims, jnp.float32)
    if shards:
        array = array * block_levels(key, dims, shards, -0.22, 0.18)
    return jnp.clip(array, -bound, bound).astype(held_as)


def setup_inputs(seed: int = 0) -> dict:
    key_of = jax.random.split(jax.random.key(seed), 10)
    prompt_keys = draw_prompt_keys(jax.random.fold_in(key_of[9], 71), 0)
    prompt_values = centred(key_of[1], (PROMPTS, PROMPT_LEN, KV_HEADS * HEAD_DIM), 1.0, 6.0, ((0, 8), (1, 4)))
    resp_queries = draw_resp_queries(jax.random.fold_in(key_of[9], 71), 0)
    resp_keys = centred(key_of[3], (PROMPTS, 2, RESP_LEN, KV_HEADS * HEAD_DIM), 1.0, 6.0, ((0, 8), (2, 4)))
    resp_values = centred(key_of[4], (PROMPTS, 2, RESP_LEN, KV_HEADS * HEAD_DIM), 1.0, 6.0, ((0, 8), (2, 4)))
    seq_grad = jnp.clip(jax.random.uniform(key_of[5], (PROMPTS, 2, RESP_LEN, QUERY_HEADS * HEAD_DIM), jnp.float32, -48.0, 48.0) * block_levels(key_of[5], (PROMPTS, 2, RESP_LEN, QUERY_HEADS * HEAD_DIM), ((0, 8), (2, 4)), -0.4, 0.0), -48.0, 48.0).astype(jnp.bfloat16)
    token_logratio = draw_token_logratio(jax.random.fold_in(key_of[9], 71), 0)
    resp_len = draw_resp_len(jax.random.fold_in(key_of[9], 71), 0)
    prefer = set_ends(jax.random.randint(key_of[8], (PROMPTS,), 0, 2), jax.random.fold_in(key_of[8], 1), 0, 1).astype(jnp.int32)
    return {"prompt_keys": prompt_keys, "prompt_values": prompt_values, "resp_queries": resp_queries, "resp_keys": resp_keys, "resp_values": resp_values, "seq_grad": seq_grad, "token_logratio": token_logratio, "resp_len": resp_len, "prefer": prefer}


BETA = 0.5

def one_response(query_rows, prompt_key_rows, prompt_value_rows, own_keys, own_values, grads_in):
    group_size = QUERY_HEADS // KV_HEADS
    scaling = 1.0 / math.sqrt(HEAD_DIM)
    key_rows = jnp.concatenate([prompt_key_rows, own_keys], 0).astype(jnp.float32).reshape(-1, KV_HEADS, HEAD_DIM)
    value_rows = jnp.concatenate([prompt_value_rows, own_values], 0).astype(jnp.float32).reshape(-1, KV_HEADS, HEAD_DIM)
    queries = query_rows.astype(jnp.float32).reshape(RESP_LEN, KV_HEADS, group_size, HEAD_DIM)
    grads_out = grads_in.astype(jnp.float32).reshape(RESP_LEN, KV_HEADS, group_size, HEAD_DIM)
    scores = jnp.einsum('tgcd,sgd->gcts', queries, key_rows) * scaling
    key_pos = jnp.arange(PROMPT_LEN + RESP_LEN, dtype=jnp.int32)
    query_pos = jnp.arange(RESP_LEN, dtype=jnp.int32)
    allowed = (key_pos[None, :] < PROMPT_LEN) | (key_pos[None, :] - PROMPT_LEN <= query_pos[:, None])
    scores = jnp.where(allowed, scores, -jnp.inf)
    maxima = lax.optimization_barrier(jnp.max(scores, axis=-1, keepdims=True))
    expanded = jnp.exp(scores - maxima)
    weights = expanded / lax.optimization_barrier(jnp.sum(expanded, axis=-1, keepdims=True))
    rounded = lax.optimization_barrier(weights.astype(jnp.bfloat16)).astype(jnp.float32)
    output = jnp.einsum('gcts,sgd->tgcd', rounded, value_rows)
    inner_sums = jnp.transpose(lax.optimization_barrier(jnp.sum(grads_out * output, axis=-1)), (1, 2, 0))
    prob_grads = jnp.einsum('tgcd,sgd->gcts', grads_out, value_rows)
    score_grads = weights * (prob_grads - inner_sums[..., None])
    rounded_grads = lax.optimization_barrier(score_grads.astype(jnp.bfloat16)).astype(jnp.float32)
    query_grads = (jnp.einsum('gcts,sgd->tgcd', rounded_grads, key_rows) * scaling).reshape(RESP_LEN, -1)
    key_grads = (jnp.einsum('gcts,tgcd->sgd', rounded_grads, queries) * scaling).reshape(-1, KV_HEADS * HEAD_DIM)
    value_grads = jnp.einsum('gcts,tgcd->sgd', rounded, grads_out).reshape(-1, KV_HEADS * HEAD_DIM)
    return (query_grads, key_grads, value_grads)

def reference(prompt_keys, prompt_values, resp_queries, resp_keys, resp_values, seq_grad, token_logratio, resp_len, prefer):
    alive_mask = jnp.arange(RESP_LEN, dtype=jnp.int32)[None, None, :] < resp_len[:, :, None]
    ratio_sums = lax.optimization_barrier(jnp.sum(jnp.where(alive_mask, token_logratio, 0.0), axis=2))
    partner = (jnp.arange(PROMPTS, dtype=jnp.int32) + PROMPTS // 2) % PROMPTS
    pref_sign = jnp.where(prefer == 1, 1.0, -1.0).astype(jnp.float32)
    margin = BETA * pref_sign * (ratio_sums[:, 0] - ratio_sums[partner, 1])
    losses = jax.nn.softplus(-margin)
    weight = BETA * pref_sign * jax.nn.sigmoid(-margin)
    factors = jnp.stack([-weight, weight[partner]], axis=1)
    cotangent = (factors[:, :, None, None] * jnp.where(alive_mask[..., None], seq_grad.astype(jnp.float32), 0.0)).astype(jnp.bfloat16)
    source = jnp.stack([jnp.arange(PROMPTS, dtype=jnp.int32), partner], axis=1).reshape(-1)

    def per_response(pieces):
        prompt_row, query_rows, own_keys, own_values, grads_in = pieces
        chosen_keys = lax.dynamic_index_in_dim(prompt_keys, prompt_row, 0, keepdims=False)
        chosen_values = lax.dynamic_index_in_dim(prompt_values, prompt_row, 0, keepdims=False)
        return one_response(query_rows, chosen_keys, chosen_values, own_keys, own_values, grads_in)
    query_grads, key_grads, value_grads = lax.map(per_response, (source, resp_queries.reshape(2 * PROMPTS, RESP_LEN, -1), resp_keys.reshape(2 * PROMPTS, RESP_LEN, -1), resp_values.reshape(2 * PROMPTS, RESP_LEN, -1), cotangent.reshape(2 * PROMPTS, RESP_LEN, -1)))
    key_grads = key_grads.reshape(PROMPTS, 2, PROMPT_LEN + RESP_LEN, -1)
    value_grads = value_grads.reshape(PROMPTS, 2, PROMPT_LEN + RESP_LEN, -1)
    prompt_dk = key_grads[:, 0, :PROMPT_LEN] + key_grads[partner, 1, :PROMPT_LEN]
    prompt_dv = value_grads[:, 0, :PROMPT_LEN] + value_grads[partner, 1, :PROMPT_LEN]
    resp_dq = query_grads.reshape(PROMPTS, 2, RESP_LEN, -1)
    return (prompt_dk, prompt_dv, resp_dq, key_grads[:, :, PROMPT_LEN:], value_grads[:, :, PROMPT_LEN:], losses)
```

```python
import functools
import math

import jax
import jax.numpy as jnp
from jax import lax
from jax.experimental import pallas as pl
from jax.experimental.pallas import tpu as pltpu
from jax.sharding import PartitionSpec as P

HEAD_DIM = 128
QUERY_HEADS = 16
KV_HEADS = 4
GROUP = QUERY_HEADS // KV_HEADS
BLOCK_LEN = 128
BETA = 0.5
SCALING = 1.0 / math.sqrt(HEAD_DIM)
EXP2_SCALING = SCALING * math.log2(math.e)
CHUNK = 512
EXTRA = 16
VMEM_LIMIT = 48 * 2**20
F32 = jnp.float32
BF16 = jnp.bfloat16


def dot(left, right, left_dim, right_dim):
    return lax.dot_general(
        left, right, (((left_dim,), (right_dim,)), ((), ())), preferred_element_type=F32
    )


def vmem():
    return pl.BlockSpec(memory_space=pltpu.VMEM)


def smem():
    return pl.BlockSpec(memory_space=pltpu.SMEM)


def params():
    return pltpu.CompilerParams(vmem_limit_bytes=VMEM_LIMIT)


def columns(seq, k, width, sharing=1):
    return pl.ds(pl.multiple_of((seq ^ k) // sharing * width, width), width)


def split_float(value):
    high = value.astype(BF16)
    rest = value - high.astype(F32)
    middle = rest.astype(BF16)
    low = (rest - middle.astype(F32)).astype(BF16)
    return high, middle, low


def join_float(rows, at):
    terms = [rows[at + i : at + i + 1, :].astype(F32) for i in range(3)]
    return terms[0] + terms[1] + terms[2]


def write_sums(target, sums, first_row):
    rows = [term.astype(F32) for value in sums for term in split_float(value)]
    rows += [jnp.zeros_like(rows[0])] * (EXTRA - len(rows))
    target[pl.ds(first_row, EXTRA), :] = jnp.concatenate(rows, axis=0).astype(BF16)


def pack_prompt_body(info, keys, values, ratios, *blocks):
    seq = info[0]
    rows = keys.shape[1]
    tokens = ratios.shape[2]
    width = 2 * HEAD_DIM
    sharing = len(blocks) // KV_HEADS
    positions = seq * tokens + lax.broadcasted_iota(jnp.int32, (1, tokens), 1)
    sums = []
    for slot in range(2):
        alive = positions < info[1 + slot]
        total = jnp.sum(
            jnp.where(alive, ratios[0, slot : slot + 1, :], 0.0), axis=1, keepdims=True
        )
        sums.append(jnp.broadcast_to(total, (1, width)))
    for k, block in enumerate(blocks):
        head = columns(seq, k, HEAD_DIM, sharing)
        block[0:rows, 0:HEAD_DIM] = keys[0, :, head]
        block[0:rows, HEAD_DIM:width] = values[0, :, head]
        write_sums(block, sums, rows)


def pack_prompt(count, info, keys, values, ratios):
    shape = jax.ShapeDtypeStruct((keys.shape[1] + EXTRA, 2 * HEAD_DIM), BF16)
    return pl.pallas_call(
        pack_prompt_body,
        out_shape=[shape] * count,
        in_specs=[smem(), vmem(), vmem(), vmem()],
        out_specs=[vmem()] * count,
        compiler_params=params(),
    )(info, keys, values, ratios)


def join_prompt_body(*refs):
    *blocks, joined = refs
    rows = blocks[0].shape[0] - EXTRA
    sums = [None, None]
    for k, block in enumerate(blocks):
        joined[k * rows : (k + 1) * rows, :] = block[0:rows, :]
        extra = block[rows : rows + EXTRA, :]
        for slot in range(2):
            value = join_float(extra, 3 * slot)
            sums[slot] = value if sums[slot] is None else sums[slot] + value
    write_sums(joined, sums, len(blocks) * rows)


def join_prompt(blocks):
    rows = blocks[0].shape[0] - EXTRA
    return pl.pallas_call(
        join_prompt_body,
        out_shape=jax.ShapeDtypeStruct((len(blocks) * rows + EXTRA, 2 * HEAD_DIM), BF16),
        in_specs=[vmem()] * len(blocks),
        out_specs=vmem(),
        compiler_params=params(),
    )(*blocks)


def pack_slot_body(info, queries, grads, keys, values, *blocks):
    seq = info[0]
    sharing = len(blocks) // KV_HEADS
    width = queries.shape[3] // len(blocks)
    at = 2 * width
    for k, block in enumerate(blocks):
        heads = columns(seq, k, width)
        block[:, 0:width] = queries[0, 0, :, heads]
        block[:, width:at] = grads[0, 0, :, heads]
        head = columns(seq, k, HEAD_DIM, sharing)
        block[:, at : at + HEAD_DIM] = keys[0, 0, :, head]
        block[:, at + HEAD_DIM :] = values[0, 0, :, head]


def pack_slot(slot, count, info, queries, grads, keys, values):
    tokens = queries.shape[2]
    wide = pl.BlockSpec((1, 1, tokens, queries.shape[3]), lambda i: (0, slot, 0, 0))
    narrow = pl.BlockSpec((1, 1, tokens, keys.shape[3]), lambda i: (0, slot, 0, 0))
    width = 2 * queries.shape[3] // count + 2 * HEAD_DIM
    block = pl.BlockSpec((tokens, width), lambda i: (0, 0))
    return pl.pallas_call(
        pack_slot_body,
        grid=(1,),
        out_shape=[jax.ShapeDtypeStruct((tokens, width), BF16)] * count,
        in_specs=[smem(), wide, wide, narrow, narrow],
        out_specs=[block] * count,
        compiler_params=params(),
    )(info, queries, grads, keys, values)


def slot_body(slot, count, info, prompt, other, *refs):
    blocks, outs = refs[0:count], refs[count : 2 * count]
    prompt_grads, losses, *scratch = refs[2 * count :]
    q_all, c_all, k_all, v_all, weights, probs, dk, dv, dq_all = scratch
    seq, length = info[0], info[1 + slot]
    prompt_rows = prompt.shape[0] - EXTRA
    shard = blocks[0].shape[0]
    tokens = count * shard
    heads = GROUP * KV_HEADS // count
    width = heads * HEAD_DIM
    rows_per_tile = heads * BLOCK_LEN
    keys = prompt_rows + tokens

    near = prompt[prompt_rows : prompt_rows + EXTRA, 0:HEAD_DIM]
    far = other[:, 0:HEAD_DIM]
    if slot == 1:
        near, far = far, near
    own_sign = jnp.where(info[3] == 1, 1.0, -1.0)
    partner_sign = jnp.where(info[4] == 1, 1.0, -1.0)
    own_margin = BETA * own_sign * (join_float(near, 0) - join_float(far, 3))
    partner_margin = BETA * partner_sign * (join_float(far, 0) - join_float(near, 3))
    if slot == 0:
        factor = -(BETA * own_sign / (1.0 + jnp.exp(own_margin)))
    else:
        factor = BETA * partner_sign / (1.0 + jnp.exp(partner_margin))
    losses[...] = jnp.maximum(-own_margin, 0.0) + jnp.log1p(jnp.exp(-jnp.abs(own_margin)))

    k_all[0:prompt_rows, :] = prompt[0:prompt_rows, 0:HEAD_DIM]
    v_all[0:prompt_rows, :] = prompt[0:prompt_rows, HEAD_DIM:]
    at = 2 * width
    for k, block in enumerate(blocks):
        base = pl.multiple_of((seq ^ k) * shard, shard)
        positions = base + lax.broadcasted_iota(jnp.int32, (shard, HEAD_DIM), 0)
        scale = jnp.where(positions < length, factor, 0.0)
        for u in range(shard // BLOCK_LEN):
            part = slice(u * BLOCK_LEN, (u + 1) * BLOCK_LEN)
            for g in range(heads):
                row = pl.multiple_of(base * heads + (u * heads + g) * BLOCK_LEN, BLOCK_LEN)
                rows = pl.ds(row, BLOCK_LEN)
                head = g * HEAD_DIM
                q_all[rows, :] = block[part, head : head + HEAD_DIM]
                head = width + g * HEAD_DIM
                grad = block[part, head : head + HEAD_DIM].astype(F32)
                c_all[rows, :] = (scale[part] * grad).astype(BF16)
        rows = pl.ds(pl.multiple_of(prompt_rows + base, shard), shard)
        k_all[rows, :] = block[:, at : at + HEAD_DIM]
        v_all[rows, :] = block[:, at + HEAD_DIM :]

    dk[...] = jnp.zeros_like(dk)
    dv[...] = jnp.zeros_like(dv)
    spans = [slice(i * CHUNK, (i + 1) * CHUNK) for i in range(keys // CHUNK)]

    def tile(number, carry):
        rows = pl.ds(pl.multiple_of(number * rows_per_tile, rows_per_tile), rows_per_tile)

        @pl.when(number * BLOCK_LEN < length)
        def live():
            queries, grads = q_all[rows, :], c_all[rows, :]
            lane = lax.broadcasted_iota(jnp.int32, (1, rows_per_tile), 1)
            positions = number * BLOCK_LEN + lane % BLOCK_LEN
            maxima = totals = inner = dq = None
            for span in spans:
                scores = dot(k_all[span, :], queries, 1, 1)
                if span.stop > prompt_rows:
                    key = span.start - prompt_rows
                    key = key + lax.broadcasted_iota(jnp.int32, (CHUNK, 1), 0)
                    scores = jnp.where(key <= positions, scores, -jnp.inf)
                weights[span, :] = scores
                top = jnp.max(scores, axis=0, keepdims=True)
                maxima = top if maxima is None else jnp.maximum(maxima, top)
            for span in spans:
                part = jnp.exp2((weights[span, :] - maxima) * EXP2_SCALING)
                weights[span, :] = part
                total = jnp.sum(part, axis=0, keepdims=True)
                totals = total if totals is None else totals + total
            inverse = 1.0 / totals
            for span in spans:
                rounded = (weights[span, :] * inverse).astype(BF16)
                grad = dot(v_all[span, :], grads, 1, 1)
                probs[span, :] = grad
                part = jnp.sum(rounded.astype(F32) * grad, axis=0, keepdims=True)
                inner = part if inner is None else inner + part
                dv[span, :] += dot(rounded, grads, 1, 0)
            for span in spans:
                scores = (weights[span, :] * inverse * (probs[span, :] - inner)).astype(BF16)
                dk[span, :] += dot(scores, queries, 1, 0)
                part = dot(scores, k_all[span, :], 0, 0)
                dq = part if dq is None else dq + part
            dq_all[rows, :] = dq * SCALING

        @pl.when(number * BLOCK_LEN >= length)
        def dead():
            dq_all[rows, :] = jnp.zeros((rows_per_tile, HEAD_DIM), F32)

        return carry

    lax.fori_loop(0, tokens // BLOCK_LEN, tile, 0)

    for k, out in enumerate(outs):
        base = pl.multiple_of((seq ^ k) * shard, shard)
        for u in range(shard // BLOCK_LEN):
            part = slice(u * BLOCK_LEN, (u + 1) * BLOCK_LEN)
            for g in range(heads):
                row = pl.multiple_of(base * heads + (u * heads + g) * BLOCK_LEN, BLOCK_LEN)
                head = g * HEAD_DIM
                out[part, head : head + HEAD_DIM] = dq_all[pl.ds(row, BLOCK_LEN), :].astype(
                    out.dtype
                )
        rows = pl.ds(pl.multiple_of(prompt_rows + base, shard), shard)
        out[:, width : width + HEAD_DIM] = (dk[rows, :] * SCALING).astype(out.dtype)
        out[:, width + HEAD_DIM :] = dv[rows, :].astype(out.dtype)
    prompt_grads[:, 0:HEAD_DIM] = (dk[0:prompt_rows, :] * SCALING).astype(prompt_grads.dtype)
    prompt_grads[:, HEAD_DIM:] = dv[0:prompt_rows, :].astype(prompt_grads.dtype)


def slot_grads(slot, info, prompt, other, blocks):
    prompt_rows = prompt.shape[0] - EXTRA
    count = len(blocks)
    shard = blocks[0].shape[0]
    tokens = count * shard
    keys = prompt_rows + tokens
    heads = GROUP * KV_HEADS // count
    rows = heads * tokens
    rows_per_tile = heads * BLOCK_LEN
    width = (heads + 2) * HEAD_DIM
    out_shape = [jax.ShapeDtypeStruct((shard, width), F32)]
    out_shape += [jax.ShapeDtypeStruct((shard, width), BF16)] * (count - 1)
    out_shape += [
        jax.ShapeDtypeStruct((prompt_rows, 2 * HEAD_DIM), F32 if slot == 0 else BF16),
        jax.ShapeDtypeStruct((1, HEAD_DIM), F32),
    ]

    def whole(shape):
        return pl.BlockSpec(shape, lambda i: (0, 0))

    last = pl.BlockSpec((EXTRA, 2 * HEAD_DIM), lambda i: (prompt_rows // EXTRA, 0))
    in_specs = [smem(), whole(prompt.shape), last] + [whole(b.shape) for b in blocks]
    return pl.pallas_call(
        functools.partial(slot_body, slot, count),
        grid=(1,),
        out_shape=out_shape,
        in_specs=in_specs,
        out_specs=[whole(s.shape) for s in out_shape],
        scratch_shapes=[
            pltpu.VMEM((rows, HEAD_DIM), BF16),
            pltpu.VMEM((rows, HEAD_DIM), BF16),
            pltpu.VMEM((keys, HEAD_DIM), BF16),
            pltpu.VMEM((keys, HEAD_DIM), BF16),
            pltpu.VMEM((keys, rows_per_tile), F32),
            pltpu.VMEM((keys, rows_per_tile), F32),
            pltpu.VMEM((keys, HEAD_DIM), F32),
            pltpu.VMEM((keys, HEAD_DIM), F32),
            pltpu.VMEM((rows, HEAD_DIM), F32),
        ],
        compiler_params=params(),
        cost_estimate=pl.CostEstimate(
            flops=10 * rows * keys * HEAD_DIM,
            bytes_accessed=4 * 2**20,
            transcendentals=rows * keys,
        ),
    )(info, prompt, other, *blocks)


def add_body(near, far, *outs):
    rows = outs[0].shape[0]
    for k, out in enumerate(outs):
        part = slice(k * rows, (k + 1) * rows)
        out[...] = (near[part, :] + far[part, :].astype(F32)).astype(out.dtype)


def add_prompt(count, near, far):
    rows = near.shape[0] // count
    out_shape = [jax.ShapeDtypeStruct((rows, 2 * HEAD_DIM), F32)]
    out_shape += [jax.ShapeDtypeStruct((rows, 2 * HEAD_DIM), BF16)] * (count - 1)
    return pl.pallas_call(
        add_body,
        out_shape=out_shape,
        in_specs=[vmem()] * 2,
        out_specs=[vmem()] * count,
        compiler_params=params(),
    )(near, far)


def spread_body(count, info, *refs):
    seq = info[0]
    sharing = count // KV_HEADS
    slots, prompt = (refs[0:count], refs[count : 2 * count]), refs[2 * count : 3 * count]
    prompt_dk, prompt_dv, resp_dq, resp_dk, resp_dv = refs[3 * count :]
    at = resp_dq.shape[3] // count

    def head_sum(blocks, k, first):
        part = slice(first, first + HEAD_DIM)
        total = blocks[k][:, part].astype(F32)
        for i in range(1, sharing):
            total = total + blocks[k + i][:, part].astype(F32)
        return total

    for slot, blocks in enumerate(slots):
        for k, block in enumerate(blocks):
            resp_dq[0, slot, :, columns(seq, k, at)] = block[:, 0:at].astype(F32)
        for k in range(0, count, sharing):
            head = columns(seq, k, HEAD_DIM, sharing)
            resp_dk[0, slot, :, head] = head_sum(blocks, k, at)
            resp_dv[0, slot, :, head] = head_sum(blocks, k, at + HEAD_DIM)
    for k in range(0, count, sharing):
        head = columns(seq, k, HEAD_DIM, sharing)
        prompt_dk[0, :, head] = head_sum(prompt, k, 0)
        prompt_dv[0, :, head] = head_sum(prompt, k, HEAD_DIM)


def spread(info, slot_blocks, prompt_blocks):
    count = len(prompt_blocks)
    shard = slot_blocks[0][0].shape[0]
    rows = prompt_blocks[0].shape[0]
    kv_width = KV_HEADS * HEAD_DIM
    out_shape = [jax.ShapeDtypeStruct((1, rows, kv_width), F32)] * 2
    out_shape += [jax.ShapeDtypeStruct((1, 2, shard, QUERY_HEADS * HEAD_DIM), F32)]
    out_shape += [jax.ShapeDtypeStruct((1, 2, shard, kv_width), F32)] * 2
    return pl.pallas_call(
        functools.partial(spread_body, count),
        out_shape=out_shape,
        in_specs=[smem()] + [vmem()] * (3 * count),
        out_specs=[vmem()] * 5,
        compiler_params=params(),
    )(info, *slot_blocks[0], *slot_blocks[1], *prompt_blocks)


def exchange(blocks):
    count = len(blocks)
    received = [blocks[0]]
    for k in range(1, count):
        received.append(lax.ppermute(blocks[k], "seq", [(i, i ^ k) for i in range(count)]))
    return received


def partner(x):
    count = lax.axis_size("pair")
    return lax.ppermute(x, "pair", [(i, i ^ count // 2) for i in range(count)])


def after(x, *earlier):
    return lax.optimization_barrier((x, earlier))[0]


def on_device(
    prompt_keys,
    prompt_values,
    resp_queries,
    resp_keys,
    resp_values,
    seq_grad,
    token_logratio,
    resp_len,
    prefer,
):
    count = lax.axis_size("seq")
    pair_count = lax.axis_size("pair")
    pair_index = lax.axis_index("pair")
    partner_index = pair_index ^ pair_count // 2
    info = jnp.stack(
        [
            lax.axis_index("seq").astype(jnp.int32),
            resp_len[0, 0],
            resp_len[0, 1],
            lax.dynamic_index_in_dim(prefer, pair_index, 0, keepdims=False),
            lax.dynamic_index_in_dim(prefer, partner_index, 0, keepdims=False),
        ]
    )
    slot_args = (resp_queries, seq_grad, resp_keys, resp_values)
    prompt_blocks = exchange(pack_prompt(count, info, prompt_keys, prompt_values, token_logratio))
    blocks_1 = exchange(pack_slot(1, count, info, *slot_args))
    near = join_prompt(prompt_blocks)
    far = partner(near)
    blocks_0 = exchange(pack_slot(0, count, after(info, near), *slot_args))
    *outs_1, share, _ = slot_grads(1, info, far, near, blocks_1)
    returned = partner(share)
    outs_1 = exchange(outs_1)
    *outs_0, kept, losses = slot_grads(0, after(info, share), near, far, blocks_0)
    outs_0 = exchange(outs_0)
    prompt_grads = exchange(add_prompt(count, kept, returned))
    outs = spread(info, (outs_0, outs_1), prompt_grads)
    return (*outs, losses[0, 0:1])


def solution(mesh):
    in_specs = (
        P("pair", "seq", None),
        P("pair", "seq", None),
        P("pair", None, "seq", None),
        P("pair", None, "seq", None),
        P("pair", None, "seq", None),
        P("pair", None, "seq", None),
        P("pair", None, "seq"),
        P("pair", None),
        P(),
    )
    out_specs = (
        P("pair", "seq", None),
        P("pair", "seq", None),
        P("pair", None, "seq", None),
        P("pair", None, "seq", None),
        P("pair", None, "seq", None),
        P("pair"),
    )
    return jax.shard_map(
        on_device, mesh=mesh, in_specs=in_specs, out_specs=out_specs, check_vma=False
    )
```

```python
import functools
import math

import jax
import jax.numpy as jnp
from jax import lax
from jax.experimental import pallas as pl
from jax.experimental.pallas import tpu as pltpu
from jax.sharding import PartitionSpec as P

HEAD_DIM = 128
QUERY_HEADS = 16
KV_HEADS = 4
GROUP = QUERY_HEADS // KV_HEADS
BLOCK_LEN = 128
BETA = 0.5
SCALING = 1.0 / math.sqrt(HEAD_DIM)
EXP2_SCALING = SCALING * math.log2(math.e)
CHUNK = 512
EXTRA = 16
VMEM_LIMIT = 24 * 2**20
VMEM_ALL = 60 * 2**20
F32 = jnp.float32
BF16 = jnp.bfloat16


def dot(left, right, left_dim, right_dim):
    return lax.dot_general(
        left, right, (((left_dim,), (right_dim,)), ((), ())), preferred_element_type=F32
    )


def vmem():
    return pl.BlockSpec(memory_space=pltpu.VMEM)


def smem():
    return pl.BlockSpec(memory_space=pltpu.SMEM)


def whole(x):
    return pl.BlockSpec(x.shape, lambda i: (0,) * len(x.shape))


def params(limit=VMEM_LIMIT):
    return pltpu.CompilerParams(vmem_limit_bytes=limit)


def columns(seq, k, width, sharing=1):
    return pl.ds(pl.multiple_of((seq ^ k) // sharing * width, width), width)


def split_float(value):
    high = value.astype(BF16)
    rest = value - high.astype(F32)
    middle = rest.astype(BF16)
    low = (rest - middle.astype(F32)).astype(BF16)
    return high, middle, low


def join_float(rows, at):
    terms = [rows[at + i : at + i + 1, :].astype(F32) for i in range(3)]
    return terms[0] + terms[1] + terms[2]


def write_sums(target, sums, first_row):
    rows = [term.astype(F32) for value in sums for term in split_float(value)]
    rows += [jnp.zeros_like(rows[0])] * (EXTRA - len(rows))
    target[pl.ds(first_row, EXTRA), :] = jnp.concatenate(rows, axis=0).astype(BF16)


def pack_prompt_body(lengths, keys, values, ratios, *blocks):
    seq = lax.axis_index("seq")
    rows = keys.shape[1]
    tokens = ratios.shape[2]
    width = 2 * HEAD_DIM
    sharing = len(blocks) // KV_HEADS
    positions = seq * tokens + lax.broadcasted_iota(jnp.int32, (1, tokens), 1)
    sums = []
    for slot in range(2):
        alive = positions < lengths[0, slot]
        total = jnp.sum(
            jnp.where(alive, ratios[0, slot : slot + 1, :], 0.0), axis=1, keepdims=True
        )
        sums.append(jnp.broadcast_to(total, (1, width)))
    for k, block in enumerate(blocks):
        head = columns(seq, k, HEAD_DIM, sharing)
        block[0:rows, 0:HEAD_DIM] = keys[0, :, head]
        block[0:rows, HEAD_DIM:width] = values[0, :, head]
        write_sums(block, sums, rows)


def pack_prompt(count, lengths, keys, values, ratios):
    shape = jax.ShapeDtypeStruct((keys.shape[1] + EXTRA, 2 * HEAD_DIM), BF16)
    return pl.pallas_call(
        pack_prompt_body,
        grid=(1,),
        out_shape=[shape] * count,
        in_specs=[smem(), whole(keys), whole(values), whole(ratios)],
        out_specs=[whole(shape)] * count,
        compiler_params=params(VMEM_ALL),
    )(lengths, keys, values, ratios)


def join_prompt_body(*refs):
    *blocks, joined_keys, joined_values = refs
    rows = blocks[0].shape[0] - EXTRA
    sums = [None, None]
    for k, block in enumerate(blocks):
        part = slice(k * rows, (k + 1) * rows)
        joined_keys[part, :] = block[0:rows, 0:HEAD_DIM]
        joined_values[part, :] = block[0:rows, HEAD_DIM:]
        extra = block[rows : rows + EXTRA, 0:HEAD_DIM]
        for slot in range(2):
            value = join_float(extra, 3 * slot)
            sums[slot] = value if sums[slot] is None else sums[slot] + value
    write_sums(joined_keys, sums, len(blocks) * rows)


def join_prompt(blocks):
    rows = len(blocks) * (blocks[0].shape[0] - EXTRA)
    return pl.pallas_call(
        join_prompt_body,
        out_shape=[
            jax.ShapeDtypeStruct((rows + EXTRA, HEAD_DIM), BF16),
            jax.ShapeDtypeStruct((rows, HEAD_DIM), BF16),
        ],
        in_specs=[vmem()] * len(blocks),
        out_specs=[vmem()] * 2,
        compiler_params=params(),
    )(*blocks)


def pack_slot_body(lengths, queries, grads, keys, values, *blocks):
    seq = lax.axis_index("seq")
    sharing = len(blocks) // KV_HEADS
    width = queries.shape[3] // len(blocks)
    at = 2 * width
    for k, block in enumerate(blocks):
        heads = columns(seq, k, width)
        block[:, 0:width] = queries[0, 0, :, heads]
        block[:, width:at] = grads[0, 0, :, heads]
        head = columns(seq, k, HEAD_DIM, sharing)
        block[:, at : at + HEAD_DIM] = keys[0, 0, :, head]
        block[:, at + HEAD_DIM :] = values[0, 0, :, head]


def pack_slot(slot, count, lengths, queries, grads, keys, values):
    tokens = queries.shape[2]
    wide = pl.BlockSpec((1, 1, tokens, queries.shape[3]), lambda i: (0, slot, 0, 0))
    narrow = pl.BlockSpec((1, 1, tokens, keys.shape[3]), lambda i: (0, slot, 0, 0))
    width = 2 * queries.shape[3] // count + 2 * HEAD_DIM
    block = pl.BlockSpec((tokens, width), lambda i: (0, 0))
    return pl.pallas_call(
        pack_slot_body,
        grid=(1,),
        out_shape=[jax.ShapeDtypeStruct((tokens, width), BF16)] * count,
        in_specs=[smem(), wide, wide, narrow, narrow],
        out_specs=[block] * count,
        compiler_params=params(VMEM_ALL),
    )(lengths, queries, grads, keys, values)


class Sizes:
    def __init__(self, count, prompt_rows, shard):
        self.count, self.prompt_rows, self.shard = count, prompt_rows, shard
        self.tokens = count * shard
        self.keys = prompt_rows + self.tokens
        self.heads = GROUP * KV_HEADS // count
        self.width = self.heads * HEAD_DIM
        self.tile_rows = self.heads * BLOCK_LEN
        self.tiles = self.tokens // BLOCK_LEN
        self.rows = self.heads * self.tokens

    def tile(self, number):
        return slice(number * self.tile_rows, (number + 1) * self.tile_rows)

    def spans(self, tile):
        end = self.prompt_rows + (tile + 1) * BLOCK_LEN
        cuts = list(range(0, self.prompt_rows, CHUNK))
        cuts += list(range(self.prompt_rows, end, CHUNK)) + [end]
        return [slice(a, b) for a, b in zip(cuts, cuts[1:])]

    def own_rows(self, seq, k):
        base = pl.multiple_of((seq ^ k) * self.shard, self.shard)
        places = []
        for u in range(self.shard // BLOCK_LEN):
            for g in range(self.heads):
                row = base * self.heads + (u * self.heads + g) * BLOCK_LEN
                rows = pl.ds(pl.multiple_of(row, BLOCK_LEN), BLOCK_LEN)
                places.append((slice(u * BLOCK_LEN, (u + 1) * BLOCK_LEN), g, rows))
        return base, places

    def resp_rows(self, base):
        return pl.ds(pl.multiple_of(self.prompt_rows + base, self.shard), self.shard)


def preference(slot, prefer, near, far):
    pair = lax.axis_index("pair")
    partner_index = pair ^ (lax.axis_size("pair") // 2)
    own_sign = jnp.where(prefer[pair] == 1, 1.0, -1.0)
    partner_sign = jnp.where(prefer[partner_index] == 1, 1.0, -1.0)
    own_margin = BETA * own_sign * (join_float(near, 0) - join_float(far, 3))
    partner_margin = BETA * partner_sign * (join_float(far, 0) - join_float(near, 3))
    if slot == 0:
        factor = -(BETA * own_sign / (1.0 + jnp.exp(own_margin)))
    else:
        factor = BETA * partner_sign / (1.0 + jnp.exp(partner_margin))
    loss = jnp.maximum(-own_margin, 0.0) + jnp.log1p(jnp.exp(-jnp.abs(own_margin)))
    return factor, loss


def load_tokens(sizes, length, factor, prompt, blocks, queries, grads, keys, values):
    seq = lax.axis_index("seq")
    prompt_rows, width = sizes.prompt_rows, sizes.width
    at = 2 * width
    keys[0:prompt_rows, :] = prompt[0][0:prompt_rows, :]
    if values is not None:
        values[0:prompt_rows, :] = prompt[1][...]
    for k, block in enumerate(blocks):
        base, places = sizes.own_rows(seq, k)
        positions = base + lax.broadcasted_iota(jnp.int32, (sizes.shard, HEAD_DIM), 0)
        scale = jnp.where(positions < length, factor, 0.0)
        for part, g, rows in places:
            head = g * HEAD_DIM
            queries[rows, :] = block[part, head : head + HEAD_DIM]
            grad = block[part, width + head : width + head + HEAD_DIM].astype(F32)
            grads[rows, :] = (scale[part] * grad).astype(BF16)
        rows = sizes.resp_rows(base)
        keys[rows, :] = block[:, at : at + HEAD_DIM]
        if values is not None:
            values[rows, :] = block[:, at + HEAD_DIM :]


def masked_scores(sizes, number, span, keys, queries):
    scores = dot(keys[span, :], queries, 1, 1)
    first = span.start - sizes.prompt_rows
    if span.stop - sizes.prompt_rows > number * BLOCK_LEN + 1:
        lane = lax.broadcasted_iota(jnp.int32, (1, sizes.tile_rows), 1)
        token = number * BLOCK_LEN + lane % BLOCK_LEN
        key = first + lax.broadcasted_iota(jnp.int32, (span.stop - span.start, 1), 0)
        scores = jnp.where(key <= token, scores, -jnp.inf)
    return scores


def softmax_terms(sizes, number, spans, keys, queries, scores):
    maxima = totals = None
    for span in spans:
        part = masked_scores(sizes, number, span, keys, queries)
        scores[span, :] = part
        top = jnp.max(part, axis=0, keepdims=True)
        maxima = top if maxima is None else jnp.maximum(maxima, top)
    for span in spans:
        part = jnp.exp2((scores[span, :] - maxima) * EXP2_SCALING)
        total = jnp.sum(part, axis=0, keepdims=True)
        totals = total if totals is None else totals + total
    return maxima, 1.0 / totals


def for_tiles(sizes, length, live, dead=None):
    for number in range(sizes.tiles):
        pl.when(number * BLOCK_LEN < length)(functools.partial(live, number))
        if dead is not None:
            pl.when(number * BLOCK_LEN >= length)(functools.partial(dead, number))


def first_body(slot, sizes, lengths, prefer, keys_in, sums, *refs):
    *blocks, prompt_dv, resp_dv, stats, q_all, c_all, k_all, scores, dv = refs
    length = lengths[0, slot]
    near, far = sums[sizes.prompt_rows :, :], keys_in[sizes.prompt_rows :, :]
    factor, _ = preference(slot, prefer, near, far)
    load_tokens(sizes, length, factor, (keys_in,), blocks, q_all, c_all, k_all, None)
    dv[...] = jnp.zeros_like(dv)

    def live(number):
        rows = sizes.tile(number)
        queries, grads = q_all[rows, :], c_all[rows, :]
        spans = sizes.spans(number)
        maxima, inverse = softmax_terms(sizes, number, spans, k_all, queries, scores)
        stats[number, 0:1, :] = maxima
        stats[number, 1:2, :] = inverse
        for span in spans:
            weights = jnp.exp2((scores[span, :] - maxima) * EXP2_SCALING) * inverse
            dv[span, :] += dot(weights.astype(BF16), grads, 1, 0)

    for_tiles(sizes, length, live)
    prompt_dv[...] = dv[0 : sizes.prompt_rows, :].astype(prompt_dv.dtype)
    resp_dv[...] = dv[sizes.prompt_rows :, :]


def slot_body(slot, sizes, staged, lengths, prefer, keys_in, values_in, sums, *refs):
    count = sizes.count
    blocks, refs = refs[0:count], refs[count:]
    if staged:
        dv_in, stats, *refs = refs
    outs, refs = refs[0:count], refs[count:]
    if staged:
        prompt_dk, *scratch = refs
        q_all, c_all, k_all, v_all, scores, probs, dk, dq_all = scratch
    else:
        prompt_dk, prompt_dv, losses, *scratch = refs
        q_all, c_all, k_all, v_all, scores, probs, dk, dq_all, dv = scratch
    seq = lax.axis_index("seq")
    length = lengths[0, slot]
    prompt_rows, width = sizes.prompt_rows, sizes.width

    near, far = keys_in[prompt_rows:, :], sums[prompt_rows:, :]
    if slot == 1:
        near, far = far, near
    factor, loss = preference(slot, prefer, near, far)
    prompt = (keys_in, values_in)
    load_tokens(sizes, length, factor, prompt, blocks, q_all, c_all, k_all, v_all)
    dk[...] = jnp.zeros_like(dk)
    if not staged:
        losses[...] = loss
        dv[...] = jnp.zeros_like(dv)

    def live(number):
        rows = sizes.tile(number)
        queries, grads = q_all[rows, :], c_all[rows, :]
        spans = sizes.spans(number)
        if staged:
            maxima, inverse = stats[number, 0:1, :], stats[number, 1:2, :]
        else:
            maxima, inverse = softmax_terms(sizes, number, spans, k_all, queries, scores)

        def weights(part):
            return jnp.exp2((part - maxima) * EXP2_SCALING) * inverse

        inner = dq = None
        for span in spans:
            if staged:
                part = weights(masked_scores(sizes, number, span, k_all, queries))
                scores[span, :] = part
            else:
                part = weights(scores[span, :])
            rounded = part.astype(BF16)
            grad = dot(v_all[span, :], grads, 1, 1)
            probs[span, :] = grad
            part = jnp.sum(rounded.astype(F32) * grad, axis=0, keepdims=True)
            inner = part if inner is None else inner + part
            if not staged:
                dv[span, :] += dot(rounded, grads, 1, 0)
        for span in spans:
            part = scores[span, :] if staged else weights(scores[span, :])
            part = (part * (probs[span, :] - inner)).astype(BF16)
            dk[span, :] += dot(part, queries, 1, 0)
            part = dot(k_all[span, :], part, 0, 0)
            dq = part if dq is None else dq + part
        dq_all[rows, :] = dq.T * SCALING

    def dead(number):
        dq_all[sizes.tile(number), :] = jnp.zeros((sizes.tile_rows, HEAD_DIM), F32)

    for_tiles(sizes, length, live, dead)

    for k, out in enumerate(outs):
        base, places = sizes.own_rows(seq, k)
        for part, g, rows in places:
            head = g * HEAD_DIM
            out[part, head : head + HEAD_DIM] = dq_all[rows, :].astype(out.dtype)
        rows = sizes.resp_rows(base)
        out[:, width : width + HEAD_DIM] = (dk[rows, :] * SCALING).astype(out.dtype)
        if staged:
            part = dv_in[pl.ds(base, sizes.shard), :]
        else:
            part = dv[rows, :]
        out[:, width + HEAD_DIM :] = part.astype(out.dtype)
    prompt_dk[...] = (dk[0:prompt_rows, :] * SCALING).astype(prompt_dk.dtype)
    if not staged:
        prompt_dv[...] = dv[0:prompt_rows, :]


def cost(flops):
    return pl.CostEstimate(flops=flops, bytes_accessed=2**20, transcendentals=0)


def slot_first(slot, lengths, prefer, keys, other, blocks):
    sizes = Sizes(len(blocks), keys.shape[0] - EXTRA, blocks[0].shape[0])
    out_shape = [
        jax.ShapeDtypeStruct((sizes.prompt_rows, HEAD_DIM), BF16),
        jax.ShapeDtypeStruct((sizes.tokens, HEAD_DIM), F32),
        jax.ShapeDtypeStruct((sizes.tiles, 2, sizes.tile_rows), F32),
    ]
    return pl.pallas_call(
        functools.partial(first_body, slot, sizes),
        out_shape=out_shape,
        in_specs=[smem(), smem()] + [vmem()] * (2 + sizes.count),
        out_specs=[vmem()] * len(out_shape),
        scratch_shapes=[
            pltpu.VMEM((sizes.rows, HEAD_DIM), BF16),
            pltpu.VMEM((sizes.rows, HEAD_DIM), BF16),
            pltpu.VMEM((sizes.keys, HEAD_DIM), BF16),
            pltpu.VMEM((sizes.keys, sizes.tile_rows), F32),
            pltpu.VMEM((sizes.keys, HEAD_DIM), F32),
        ],
        compiler_params=params(),
        cost_estimate=cost(4*10**9),
    )(lengths, prefer, keys, other, *blocks)


def slot_grads(slot, lengths, prefer, prompt, other, blocks, staged=()):
    keys, values = prompt
    sizes = Sizes(len(blocks), values.shape[0], blocks[0].shape[0])
    width = sizes.width + 2 * HEAD_DIM
    out_shape = [jax.ShapeDtypeStruct((sizes.shard, width), F32)]
    out_shape += [jax.ShapeDtypeStruct((sizes.shard, width), BF16)] * (sizes.count - 1)
    prompt_shape = (sizes.prompt_rows, HEAD_DIM)
    if staged:
        out_shape += [jax.ShapeDtypeStruct(prompt_shape, BF16)]
    else:
        out_shape += [jax.ShapeDtypeStruct(prompt_shape, F32)] * 2
        out_shape += [jax.ShapeDtypeStruct((1, HEAD_DIM), F32)]
    in_specs = [smem(), smem()] + [vmem()] * (3 + sizes.count + len(staged))
    scratch = [
        pltpu.VMEM((sizes.rows, HEAD_DIM), BF16),
        pltpu.VMEM((sizes.rows, HEAD_DIM), BF16),
        pltpu.VMEM((sizes.keys, HEAD_DIM), BF16),
        pltpu.VMEM((sizes.keys, HEAD_DIM), BF16),
        pltpu.VMEM((sizes.keys, sizes.tile_rows), F32),
        pltpu.VMEM((sizes.keys, sizes.tile_rows), F32),
        pltpu.VMEM((sizes.keys, HEAD_DIM), F32),
        pltpu.VMEM((sizes.rows, HEAD_DIM), F32),
    ]
    if not staged:
        scratch += [pltpu.VMEM((sizes.keys, HEAD_DIM), F32)]
    return pl.pallas_call(
        functools.partial(slot_body, slot, sizes, bool(staged)),
        out_shape=out_shape,
        in_specs=in_specs,
        out_specs=[vmem()] * len(out_shape),
        scratch_shapes=scratch,
        compiler_params=params(),
        cost_estimate=cost(4*10**9 if staged else 4*10**9),
    )(lengths, prefer, keys, values, other, *blocks, *staged)


def add_body(near_keys, near_values, far_keys, far_values, *outs):
    rows = outs[0].shape[0]
    for k, out in enumerate(outs):
        part = slice(k * rows, (k + 1) * rows)
        total = near_keys[part, :] + far_keys[part, :].astype(F32)
        out[:, 0:HEAD_DIM] = total.astype(out.dtype)
        total = near_values[part, :] + far_values[part, :].astype(F32)
        out[:, HEAD_DIM:] = total.astype(out.dtype)


def add_prompt(count, *terms):
    rows = terms[0].shape[0] // count
    out_shape = [jax.ShapeDtypeStruct((rows, 2 * HEAD_DIM), F32)]
    out_shape += [jax.ShapeDtypeStruct((rows, 2 * HEAD_DIM), BF16)] * (count - 1)
    return pl.pallas_call(
        add_body,
        out_shape=out_shape,
        in_specs=[vmem()] * 4,
        out_specs=[vmem()] * count,
        compiler_params=params(),
    )(*terms)


def head_sum(blocks, k, first):
    part = slice(first, first + HEAD_DIM)
    total = blocks[k][:, part].astype(F32)
    for i in range(1, len(blocks) // KV_HEADS):
        total = total + blocks[k + i][:, part].astype(F32)
    return total


def spread_slots_body(count, *refs):
    seq = lax.axis_index("seq")
    sharing = count // KV_HEADS
    resp_dq, resp_dk, resp_dv = refs[2 * count :]
    at = resp_dq.shape[3] // count
    for slot in range(2):
        blocks = refs[slot * count : (slot + 1) * count]
        for k, block in enumerate(blocks):
            resp_dq[0, slot, :, columns(seq, k, at)] = block[:, 0:at].astype(F32)
        for k in range(0, count, sharing):
            head = columns(seq, k, HEAD_DIM, sharing)
            resp_dk[0, slot, :, head] = head_sum(blocks, k, at)
            resp_dv[0, slot, :, head] = head_sum(blocks, k, at + HEAD_DIM)


def spread_slots(blocks_0, blocks_1):
    count = len(blocks_0)
    shard = blocks_0[0].shape[0]
    kv_width = KV_HEADS * HEAD_DIM
    out_shape = [jax.ShapeDtypeStruct((1, 2, shard, QUERY_HEADS * HEAD_DIM), F32)]
    out_shape += [jax.ShapeDtypeStruct((1, 2, shard, kv_width), F32)] * 2
    return pl.pallas_call(
        functools.partial(spread_slots_body, count),
        grid=(1,),
        out_shape=out_shape,
        in_specs=[whole(b) for b in (*blocks_0, *blocks_1)],
        out_specs=[whole(s) for s in out_shape],
        compiler_params=params(),
    )(*blocks_0, *blocks_1)


def spread_prompt_body(*refs):
    seq = lax.axis_index("seq")
    *blocks, prompt_dk, prompt_dv = refs
    sharing = len(blocks) // KV_HEADS
    for k in range(0, len(blocks), sharing):
        head = columns(seq, k, HEAD_DIM, sharing)
        prompt_dk[0, :, head] = head_sum(blocks, k, 0)
        prompt_dv[0, :, head] = head_sum(blocks, k, HEAD_DIM)


def spread_prompt(blocks):
    shape = jax.ShapeDtypeStruct((1, blocks[0].shape[0], KV_HEADS * HEAD_DIM), F32)
    return pl.pallas_call(
        spread_prompt_body,
        grid=(1,),
        out_shape=[shape] * 2,
        in_specs=[whole(b) for b in blocks],
        out_specs=[whole(shape)] * 2,
        compiler_params=params(),
    )(*blocks)


def exchange(blocks):
    count = len(blocks)
    received = [blocks[0]]
    for k in range(1, count):
        received.append(lax.ppermute(blocks[k], "seq", [(i, i ^ k) for i in range(count)]))
    return received


def partner(x):
    count = lax.axis_size("pair")
    return lax.ppermute(x, "pair", [(i, i ^ count // 2) for i in range(count)])


def after(x, *earlier):
    return lax.optimization_barrier((x, earlier))[0]


def on_device(
    prompt_keys,
    prompt_values,
    resp_queries,
    resp_keys,
    resp_values,
    seq_grad,
    token_logratio,
    resp_len,
    prefer,
):
    count = lax.axis_size("seq")
    slot_args = (resp_queries, seq_grad, resp_keys, resp_values)
    packed = pack_prompt(count, resp_len, prompt_keys, prompt_values, token_logratio)
    prompt_blocks = exchange(packed)
    packed_1 = pack_slot(1, count, after(resp_len, packed), *slot_args)
    blocks_1 = exchange(packed_1)
    near_keys, near_values = join_prompt(after(prompt_blocks, packed_1[0]))
    far_keys = partner(near_keys)
    far_values = partner(near_values)
    packed_0 = pack_slot(0, count, after(resp_len, near_keys), *slot_args)
    blocks_0 = exchange(packed_0)
    lengths = after(resp_len, packed_0[0])
    share_values, *staged = slot_first(1, lengths, prefer, far_keys, near_keys, blocks_1)
    returned_values = partner(share_values)
    far = (far_keys, far_values)
    *outs_1, share_keys = slot_grads(1, lengths, prefer, far, near_keys, blocks_1, staged)
    returned_keys = partner(share_keys)
    outs_1 = exchange(outs_1)
    lengths = after(resp_len, share_keys)
    near = (near_keys, near_values)
    *outs_0, own_keys, own_values, losses = slot_grads(
        0, lengths, prefer, near, far_keys, blocks_0
    )
    outs_0 = exchange(outs_0)
    prompt_grads = exchange(
        add_prompt(count, own_keys, own_values, returned_keys, returned_values)
    )
    resp_grads = spread_slots(outs_0, outs_1)
    return (*spread_prompt(prompt_grads), *resp_grads, losses[0, 0:1])


def solution(mesh):
    in_specs = (
        P("pair", "seq", None),
        P("pair", "seq", None),
        P("pair", None, "seq", None),
        P("pair", None, "seq", None),
        P("pair", None, "seq", None),
        P("pair", None, "seq", None),
        P("pair", None, "seq"),
        P("pair", None),
        P(),
    )
    out_specs = (
        P("pair", "seq", None),
        P("pair", "seq", None),
        P("pair", None, "seq", None),
        P("pair", None, "seq", None),
        P("pair", None, "seq", None),
        P("pair"),
    )
    return jax.shard_map(
        on_device, mesh=mesh, in_specs=in_specs, out_specs=out_specs, check_vma=False
    )
```

```python
import functools
import math

import jax
import jax.numpy as jnp
from jax import lax
from jax.experimental import pallas as pl
from jax.experimental.pallas import tpu as pltpu
from jax.sharding import PartitionSpec as P

HEAD_DIM = 128
QUERY_HEADS = 16
KV_HEADS = 4
GROUP = QUERY_HEADS // KV_HEADS
BLOCK_LEN = 128
BETA = 0.5
SCALING = 1.0 / math.sqrt(HEAD_DIM)
EXP2_SCALING = SCALING * math.log2(math.e)
CHUNK = 1024
EXTRA = 16
VMEM_LIMIT = 24 * 2**20
VMEM_ALL = 60 * 2**20
F32 = jnp.float32
BF16 = jnp.bfloat16


def dot(left, right, left_dim, right_dim):
    return lax.dot_general(
        left, right, (((left_dim,), (right_dim,)), ((), ())), preferred_element_type=F32
    )


def vmem():
    return pl.BlockSpec(memory_space=pltpu.VMEM)


def smem():
    return pl.BlockSpec(memory_space=pltpu.SMEM)


def whole(x):
    return pl.BlockSpec(x.shape, lambda i: (0,) * len(x.shape))


def params(limit=VMEM_LIMIT):
    return pltpu.CompilerParams(vmem_limit_bytes=limit)


def columns(seq, k, width, sharing=1):
    return pl.ds(pl.multiple_of((seq ^ k) // sharing * width, width), width)


def split_float(value):
    high = value.astype(BF16)
    rest = value - high.astype(F32)
    middle = rest.astype(BF16)
    low = (rest - middle.astype(F32)).astype(BF16)
    return high, middle, low


def join_float(rows, at):
    terms = [rows[at + i : at + i + 1, :].astype(F32) for i in range(3)]
    return terms[0] + terms[1] + terms[2]


def write_sums(target, sums, first_row):
    rows = [term.astype(F32) for value in sums for term in split_float(value)]
    rows += [jnp.zeros_like(rows[0])] * (EXTRA - len(rows))
    target[pl.ds(first_row, EXTRA), :] = jnp.concatenate(rows, axis=0).astype(BF16)


def pack_prompt_body(lengths, keys, values, ratios, *blocks):
    seq = lax.axis_index("seq")
    rows = keys.shape[1]
    tokens = ratios.shape[2]
    width = 2 * HEAD_DIM
    sharing = len(blocks) // KV_HEADS
    positions = seq * tokens + lax.broadcasted_iota(jnp.int32, (1, tokens), 1)
    sums = []
    for slot in range(2):
        alive = positions < lengths[0, slot]
        total = jnp.sum(
            jnp.where(alive, ratios[0, slot : slot + 1, :], 0.0), axis=1, keepdims=True
        )
        sums.append(jnp.broadcast_to(total, (1, width)))
    for k, block in enumerate(blocks):
        head = columns(seq, k, HEAD_DIM, sharing)
        block[0:rows, 0:HEAD_DIM] = keys[0, :, head]
        block[0:rows, HEAD_DIM:width] = values[0, :, head]
        write_sums(block, sums, rows)


def pack_prompt(count, lengths, keys, values, ratios):
    shape = jax.ShapeDtypeStruct((keys.shape[1] + EXTRA, 2 * HEAD_DIM), BF16)
    return pl.pallas_call(
        pack_prompt_body,
        grid=(1,),
        out_shape=[shape] * count,
        in_specs=[smem(), whole(keys), whole(values), whole(ratios)],
        out_specs=[whole(shape)] * count,
        compiler_params=params(VMEM_ALL),
    )(lengths, keys, values, ratios)


def join_prompt_body(*refs):
    *blocks, joined_keys, joined_values = refs
    rows = blocks[0].shape[0] - EXTRA
    sums = [None, None]
    for k, block in enumerate(blocks):
        part = slice(k * rows, (k + 1) * rows)
        joined_keys[part, :] = block[0:rows, 0:HEAD_DIM]
        joined_values[part, :] = block[0:rows, HEAD_DIM:]
        extra = block[rows : rows + EXTRA, 0:HEAD_DIM]
        for slot in range(2):
            value = join_float(extra, 3 * slot)
            sums[slot] = value if sums[slot] is None else sums[slot] + value
    write_sums(joined_keys, sums, len(blocks) * rows)


def join_prompt(blocks):
    rows = len(blocks) * (blocks[0].shape[0] - EXTRA)
    return pl.pallas_call(
        join_prompt_body,
        out_shape=[
            jax.ShapeDtypeStruct((rows + EXTRA, HEAD_DIM), BF16),
            jax.ShapeDtypeStruct((rows, HEAD_DIM), BF16),
        ],
        in_specs=[vmem()] * len(blocks),
        out_specs=[vmem()] * 2,
        compiler_params=params(),
    )(*blocks)


def pack_slot_body(lengths, queries, grads, keys, values, *blocks):
    seq = lax.axis_index("seq")
    sharing = len(blocks) // KV_HEADS
    width = queries.shape[3] // len(blocks)
    at = 2 * width
    for k, block in enumerate(blocks):
        heads = columns(seq, k, width)
        block[:, 0:width] = queries[0, 0, :, heads]
        block[:, width:at] = grads[0, 0, :, heads]
        head = columns(seq, k, HEAD_DIM, sharing)
        block[:, at : at + HEAD_DIM] = keys[0, 0, :, head]
        block[:, at + HEAD_DIM :] = values[0, 0, :, head]


def pack_slot(slot, count, lengths, queries, grads, keys, values):
    tokens = queries.shape[2]
    wide = pl.BlockSpec((1, 1, tokens, queries.shape[3]), lambda i: (0, slot, 0, 0))
    narrow = pl.BlockSpec((1, 1, tokens, keys.shape[3]), lambda i: (0, slot, 0, 0))
    width = 2 * queries.shape[3] // count + 2 * HEAD_DIM
    block = pl.BlockSpec((tokens, width), lambda i: (0, 0))
    return pl.pallas_call(
        pack_slot_body,
        grid=(1,),
        out_shape=[jax.ShapeDtypeStruct((tokens, width), BF16)] * count,
        in_specs=[smem(), wide, wide, narrow, narrow],
        out_specs=[block] * count,
        compiler_params=params(VMEM_ALL),
    )(lengths, queries, grads, keys, values)


class Sizes:
    def __init__(self, count, prompt_rows, shard):
        self.count, self.prompt_rows, self.shard = count, prompt_rows, shard
        self.tokens = count * shard
        self.keys = prompt_rows + self.tokens
        self.heads = GROUP * KV_HEADS // count
        self.width = self.heads * HEAD_DIM
        self.tile_rows = self.heads * BLOCK_LEN
        self.tiles = self.tokens // BLOCK_LEN
        self.rows = self.heads * self.tokens

    def tile(self, number):
        return slice(number * self.tile_rows, (number + 1) * self.tile_rows)

    def spans(self, tile):
        end = self.prompt_rows + (tile + 1) * BLOCK_LEN
        cuts = list(range(0, self.prompt_rows, CHUNK))
        cuts += list(range(self.prompt_rows, end, CHUNK)) + [end]
        return [slice(a, b) for a, b in zip(cuts, cuts[1:])]

    def own_rows(self, seq, k):
        base = pl.multiple_of((seq ^ k) * self.shard, self.shard)
        places = []
        for u in range(self.shard // BLOCK_LEN):
            for g in range(self.heads):
                row = base * self.heads + (u * self.heads + g) * BLOCK_LEN
                rows = pl.ds(pl.multiple_of(row, BLOCK_LEN), BLOCK_LEN)
                places.append((slice(u * BLOCK_LEN, (u + 1) * BLOCK_LEN), g, rows))
        return base, places

    def resp_rows(self, base):
        return pl.ds(pl.multiple_of(self.prompt_rows + base, self.shard), self.shard)


def preference(slot, prefer, near, far):
    pair = lax.axis_index("pair")
    partner_index = pair ^ (lax.axis_size("pair") // 2)
    own_sign = jnp.where(prefer[pair] == 1, 1.0, -1.0)
    partner_sign = jnp.where(prefer[partner_index] == 1, 1.0, -1.0)
    own_margin = BETA * own_sign * (join_float(near, 0) - join_float(far, 3))
    partner_margin = BETA * partner_sign * (join_float(far, 0) - join_float(near, 3))
    if slot == 0:
        factor = -(BETA * own_sign / (1.0 + jnp.exp(own_margin)))
    else:
        factor = BETA * partner_sign / (1.0 + jnp.exp(partner_margin))
    loss = jnp.maximum(-own_margin, 0.0) + jnp.log1p(jnp.exp(-jnp.abs(own_margin)))
    return factor, loss


def load_tokens(sizes, length, factor, prompt, blocks, queries, grads, keys, values):
    seq = lax.axis_index("seq")
    prompt_rows, width = sizes.prompt_rows, sizes.width
    at = 2 * width
    keys[0:prompt_rows, :] = prompt[0][0:prompt_rows, :]
    if values is not None:
        values[0:prompt_rows, :] = prompt[1][...]
    for k, block in enumerate(blocks):
        base, places = sizes.own_rows(seq, k)
        positions = base + lax.broadcasted_iota(jnp.int32, (sizes.shard, HEAD_DIM), 0)
        scale = jnp.where(positions < length, factor, 0.0)
        for part, g, rows in places:
            head = g * HEAD_DIM
            queries[rows, :] = block[part, head : head + HEAD_DIM]
            grad = block[part, width + head : width + head + HEAD_DIM].astype(F32)
            grads[rows, :] = (scale[part] * grad).astype(BF16)
        rows = sizes.resp_rows(base)
        keys[rows, :] = block[:, at : at + HEAD_DIM]
        if values is not None:
            values[rows, :] = block[:, at + HEAD_DIM :]


def masked_scores(sizes, number, span, keys, queries):
    scores = dot(keys[span, :], queries, 1, 1) * EXP2_SCALING
    first = span.start - sizes.prompt_rows
    if span.stop - sizes.prompt_rows > number * BLOCK_LEN + 1:
        lane = lax.broadcasted_iota(jnp.int32, (1, sizes.tile_rows), 1)
        token = number * BLOCK_LEN + lane % BLOCK_LEN
        key = first + lax.broadcasted_iota(jnp.int32, (span.stop - span.start, 1), 0)
        scores = jnp.where(key <= token, scores, -jnp.inf)
    return scores


def softmax_terms(sizes, number, spans, keys, queries, scores):
    maxima = totals = None
    for span in spans:
        part = masked_scores(sizes, number, span, keys, queries)
        scores[span, :] = part
        top = jnp.max(part, axis=0, keepdims=True)
        maxima = top if maxima is None else jnp.maximum(maxima, top)
    for span in spans:
        part = jnp.exp2(scores[span, :] - maxima)
        total = jnp.sum(part, axis=0, keepdims=True)
        totals = total if totals is None else totals + total
    return maxima + jnp.log2(totals)


def for_tiles(sizes, length, live, dead=None):
    for number in range(sizes.tiles):
        pl.when(number * BLOCK_LEN < length)(functools.partial(live, number))
        if dead is not None:
            pl.when(number * BLOCK_LEN >= length)(functools.partial(dead, number))


def first_body(slot, sizes, lengths, prefer, keys_in, sums, *refs):
    *blocks, prompt_dv, resp_dv, stats, q_all, c_all, k_all, scores, dv = refs
    length = lengths[0, slot]
    near, far = sums[sizes.prompt_rows :, :], keys_in[sizes.prompt_rows :, :]
    factor, _ = preference(slot, prefer, near, far)
    load_tokens(sizes, length, factor, (keys_in,), blocks, q_all, c_all, k_all, None)
    dv[...] = jnp.zeros_like(dv)

    def live(number):
        rows = sizes.tile(number)
        queries, grads = q_all[rows, :], c_all[rows, :]
        spans = sizes.spans(number)
        offset = softmax_terms(sizes, number, spans, k_all, queries, scores)
        stats[number, :, :] = offset
        for span in spans:
            weights = jnp.exp2(scores[span, :] - offset)
            dv[span, :] += dot(weights.astype(BF16), grads, 1, 0)

    for_tiles(sizes, length, live)
    prompt_dv[...] = dv[0 : sizes.prompt_rows, :].astype(prompt_dv.dtype)
    resp_dv[...] = dv[sizes.prompt_rows :, :]


def slot_body(slot, sizes, staged, lengths, prefer, keys_in, values_in, sums, *refs):
    count = sizes.count
    blocks, refs = refs[0:count], refs[count:]
    if staged:
        dv_in, stats, *refs = refs
    outs, refs = refs[0:count], refs[count:]
    if staged:
        prompt_dk, *scratch = refs
        q_all, c_all, k_all, v_all, scores, probs, dk, dq_all = scratch
    else:
        prompt_dk, prompt_dv, losses, *scratch = refs
        q_all, c_all, k_all, v_all, scores, probs, dk, dq_all, dv = scratch
    seq = lax.axis_index("seq")
    length = lengths[0, slot]
    prompt_rows, width = sizes.prompt_rows, sizes.width

    near, far = keys_in[prompt_rows:, :], sums[prompt_rows:, :]
    if slot == 1:
        near, far = far, near
    factor, loss = preference(slot, prefer, near, far)
    prompt = (keys_in, values_in)
    load_tokens(sizes, length, factor, prompt, blocks, q_all, c_all, k_all, v_all)
    dk[...] = jnp.zeros_like(dk)
    if not staged:
        losses[...] = loss
        dv[...] = jnp.zeros_like(dv)

    def live(number):
        rows = sizes.tile(number)
        queries, grads = q_all[rows, :], c_all[rows, :]
        spans = sizes.spans(number)
        if staged:
            offset = stats[number, :, :]
        else:
            offset = softmax_terms(sizes, number, spans, k_all, queries, scores)
        inner = dq = None
        for span in spans:
            if staged:
                part = masked_scores(sizes, number, span, k_all, queries)
                part = jnp.exp2(part - offset)
                scores[span, :] = part
            else:
                part = jnp.exp2(scores[span, :] - offset)
            rounded = part.astype(BF16)
            grad = dot(v_all[span, :], grads, 1, 1)
            probs[span, :] = grad
            part = jnp.sum(rounded.astype(F32) * grad, axis=0, keepdims=True)
            inner = part if inner is None else inner + part
            if not staged:
                dv[span, :] += dot(rounded, grads, 1, 0)
        for span in spans:
            part = scores[span, :] if staged else jnp.exp2(scores[span, :] - offset)
            part = (part * (probs[span, :] - inner)).astype(BF16)
            dk[span, :] += dot(part, queries, 1, 0)
            part = dot(k_all[span, :], part, 0, 0)
            dq = part if dq is None else dq + part
        dq_all[rows, :] = dq.T * SCALING

    def dead(number):
        dq_all[sizes.tile(number), :] = jnp.zeros((sizes.tile_rows, HEAD_DIM), F32)

    for_tiles(sizes, length, live, dead)

    for k, out in enumerate(outs):
        base, places = sizes.own_rows(seq, k)
        for part, g, rows in places:
            head = g * HEAD_DIM
            out[part, head : head + HEAD_DIM] = dq_all[rows, :].astype(out.dtype)
        rows = sizes.resp_rows(base)
        out[:, width : width + HEAD_DIM] = (dk[rows, :] * SCALING).astype(out.dtype)
        if staged:
            part = dv_in[pl.ds(base, sizes.shard), :]
        else:
            part = dv[rows, :]
        out[:, width + HEAD_DIM :] = part.astype(out.dtype)
    prompt_dk[...] = (dk[0:prompt_rows, :] * SCALING).astype(prompt_dk.dtype)
    if not staged:
        prompt_dv[...] = dv[0:prompt_rows, :]


def cost(flops):
    return pl.CostEstimate(flops=flops, bytes_accessed=2**20, transcendentals=0)


def slot_first(slot, lengths, prefer, keys, other, blocks):
    sizes = Sizes(len(blocks), keys.shape[0] - EXTRA, blocks[0].shape[0])
    out_shape = [
        jax.ShapeDtypeStruct((sizes.prompt_rows, HEAD_DIM), BF16),
        jax.ShapeDtypeStruct((sizes.tokens, HEAD_DIM), F32),
        jax.ShapeDtypeStruct((sizes.tiles, 1, sizes.tile_rows), F32),
    ]
    return pl.pallas_call(
        functools.partial(first_body, slot, sizes),
        out_shape=out_shape,
        in_specs=[smem(), smem()] + [vmem()] * (2 + sizes.count),
        out_specs=[vmem()] * len(out_shape),
        scratch_shapes=[
            pltpu.VMEM((sizes.rows, HEAD_DIM), BF16),
            pltpu.VMEM((sizes.rows, HEAD_DIM), BF16),
            pltpu.VMEM((sizes.keys, HEAD_DIM), BF16),
            pltpu.VMEM((sizes.keys, sizes.tile_rows), F32),
            pltpu.VMEM((sizes.keys, HEAD_DIM), F32),
        ],
        compiler_params=params(),
        cost_estimate=cost(4*10**9),
    )(lengths, prefer, keys, other, *blocks)


def slot_grads(slot, lengths, prefer, prompt, other, blocks, staged=()):
    keys, values = prompt
    sizes = Sizes(len(blocks), values.shape[0], blocks[0].shape[0])
    width = sizes.width + 2 * HEAD_DIM
    out_shape = [jax.ShapeDtypeStruct((sizes.shard, width), F32)]
    out_shape += [jax.ShapeDtypeStruct((sizes.shard, width), BF16)] * (sizes.count - 1)
    prompt_shape = (sizes.prompt_rows, HEAD_DIM)
    if staged:
        out_shape += [jax.ShapeDtypeStruct(prompt_shape, BF16)]
    else:
        out_shape += [jax.ShapeDtypeStruct(prompt_shape, F32)] * 2
        out_shape += [jax.ShapeDtypeStruct((1, HEAD_DIM), F32)]
    in_specs = [smem(), smem()] + [vmem()] * (3 + sizes.count + len(staged))
    scratch = [
        pltpu.VMEM((sizes.rows, HEAD_DIM), BF16),
        pltpu.VMEM((sizes.rows, HEAD_DIM), BF16),
        pltpu.VMEM((sizes.keys, HEAD_DIM), BF16),
        pltpu.VMEM((sizes.keys, HEAD_DIM), BF16),
        pltpu.VMEM((sizes.keys, sizes.tile_rows), F32),
        pltpu.VMEM((sizes.keys, sizes.tile_rows), F32),
        pltpu.VMEM((sizes.keys, HEAD_DIM), F32),
        pltpu.VMEM((sizes.rows, HEAD_DIM), F32),
    ]
    if not staged:
        scratch += [pltpu.VMEM((sizes.keys, HEAD_DIM), F32)]
    return pl.pallas_call(
        functools.partial(slot_body, slot, sizes, bool(staged)),
        out_shape=out_shape,
        in_specs=in_specs,
        out_specs=[vmem()] * len(out_shape),
        scratch_shapes=scratch,
        compiler_params=params(),
        cost_estimate=cost(4*10**9 if staged else 4*10**9),
    )(lengths, prefer, keys, values, other, *blocks, *staged)


def add_body(near_keys, near_values, far_keys, far_values, *outs):
    rows = outs[0].shape[0]
    for k, out in enumerate(outs):
        part = slice(k * rows, (k + 1) * rows)
        total = near_keys[part, :] + far_keys[part, :].astype(F32)
        out[:, 0:HEAD_DIM] = total.astype(out.dtype)
        total = near_values[part, :] + far_values[part, :].astype(F32)
        out[:, HEAD_DIM:] = total.astype(out.dtype)


def add_prompt(count, *terms):
    rows = terms[0].shape[0] // count
    out_shape = [jax.ShapeDtypeStruct((rows, 2 * HEAD_DIM), F32)]
    out_shape += [jax.ShapeDtypeStruct((rows, 2 * HEAD_DIM), BF16)] * (count - 1)
    return pl.pallas_call(
        add_body,
        out_shape=out_shape,
        in_specs=[vmem()] * 4,
        out_specs=[vmem()] * count,
        compiler_params=params(),
    )(*terms)


def head_sum(blocks, k, first):
    part = slice(first, first + HEAD_DIM)
    total = blocks[k][:, part].astype(F32)
    for i in range(1, len(blocks) // KV_HEADS):
        total = total + blocks[k + i][:, part].astype(F32)
    return total


def spread_slots_body(count, *refs):
    seq = lax.axis_index("seq")
    sharing = count // KV_HEADS
    resp_dq, resp_dk, resp_dv = refs[2 * count :]
    at = resp_dq.shape[3] // count
    for slot in range(2):
        blocks = refs[slot * count : (slot + 1) * count]
        for k, block in enumerate(blocks):
            resp_dq[0, slot, :, columns(seq, k, at)] = block[:, 0:at].astype(F32)
        for k in range(0, count, sharing):
            head = columns(seq, k, HEAD_DIM, sharing)
            resp_dk[0, slot, :, head] = head_sum(blocks, k, at)
            resp_dv[0, slot, :, head] = head_sum(blocks, k, at + HEAD_DIM)


def spread_slots(blocks_0, blocks_1):
    count = len(blocks_0)
    shard = blocks_0[0].shape[0]
    kv_width = KV_HEADS * HEAD_DIM
    out_shape = [jax.ShapeDtypeStruct((1, 2, shard, QUERY_HEADS * HEAD_DIM), F32)]
    out_shape += [jax.ShapeDtypeStruct((1, 2, shard, kv_width), F32)] * 2
    return pl.pallas_call(
        functools.partial(spread_slots_body, count),
        grid=(1,),
        out_shape=out_shape,
        in_specs=[whole(b) for b in (*blocks_0, *blocks_1)],
        out_specs=[whole(s) for s in out_shape],
        compiler_params=params(),
    )(*blocks_0, *blocks_1)


def spread_prompt_body(*refs):
    seq = lax.axis_index("seq")
    *blocks, prompt_dk, prompt_dv = refs
    sharing = len(blocks) // KV_HEADS
    for k in range(0, len(blocks), sharing):
        head = columns(seq, k, HEAD_DIM, sharing)
        prompt_dk[0, :, head] = head_sum(blocks, k, 0)
        prompt_dv[0, :, head] = head_sum(blocks, k, HEAD_DIM)


def spread_prompt(blocks):
    shape = jax.ShapeDtypeStruct((1, blocks[0].shape[0], KV_HEADS * HEAD_DIM), F32)
    return pl.pallas_call(
        spread_prompt_body,
        grid=(1,),
        out_shape=[shape] * 2,
        in_specs=[whole(b) for b in blocks],
        out_specs=[whole(shape)] * 2,
        compiler_params=params(),
    )(*blocks)


def exchange(blocks):
    count = len(blocks)
    received = [blocks[0]]
    for k in range(1, count):
        received.append(lax.ppermute(blocks[k], "seq", [(i, i ^ k) for i in range(count)]))
    return received


def partner(x):
    count = lax.axis_size("pair")
    return lax.ppermute(x, "pair", [(i, i ^ count // 2) for i in range(count)])


def after(x, *earlier):
    return lax.optimization_barrier((x, earlier))[0]


def on_device(
    prompt_keys,
    prompt_values,
    resp_queries,
    resp_keys,
    resp_values,
    seq_grad,
    token_logratio,
    resp_len,
    prefer,
):
    count = lax.axis_size("seq")
    slot_args = (resp_queries, seq_grad, resp_keys, resp_values)
    packed = pack_prompt(count, resp_len, prompt_keys, prompt_values, token_logratio)
    prompt_blocks = exchange(packed)
    packed_1 = pack_slot(1, count, after(resp_len, packed), *slot_args)
    blocks_1 = exchange(packed_1)
    near_keys, near_values = join_prompt(after(prompt_blocks, packed_1[0]))
    far_keys = partner(near_keys)
    far_values = partner(near_values)
    packed_0 = pack_slot(0, count, after(resp_len, near_keys), *slot_args)
    blocks_0 = exchange(packed_0)
    lengths = after(resp_len, packed_0[0])
    share_values, *staged = slot_first(1, lengths, prefer, far_keys, near_keys, blocks_1)
    returned_values = partner(share_values)
    far = (far_keys, far_values)
    *outs_1, share_keys = slot_grads(1, lengths, prefer, far, near_keys, blocks_1, staged)
    returned_keys = partner(share_keys)
    outs_1 = exchange(outs_1)
    lengths = after(resp_len, share_keys)
    near = (near_keys, near_values)
    *outs_0, own_keys, own_values, losses = slot_grads(
        0, lengths, prefer, near, far_keys, blocks_0
    )
    outs_0 = exchange(outs_0)
    prompt_grads = exchange(
        add_prompt(count, own_keys, own_values, returned_keys, returned_values)
    )
    resp_grads = spread_slots(outs_0, outs_1)
    return (*spread_prompt(prompt_grads), *resp_grads, losses[0, 0:1])


def solution(mesh):
    in_specs = (
        P("pair", "seq", None),
        P("pair", "seq", None),
        P("pair", None, "seq", None),
        P("pair", None, "seq", None),
        P("pair", None, "seq", None),
        P("pair", None, "seq", None),
        P("pair", None, "seq"),
        P("pair", None),
        P(),
    )
    out_specs = (
        P("pair", "seq", None),
        P("pair", "seq", None),
        P("pair", None, "seq", None),
        P("pair", None, "seq", None),
        P("pair", None, "seq", None),
        P("pair"),
    )
    return jax.shard_map(
        on_device, mesh=mesh, in_specs=in_specs, out_specs=out_specs, check_vma=False
    )
```

```python
import functools
import math

import jax
import jax.numpy as jnp
from jax import lax
from jax.experimental import pallas as pl
from jax.experimental.pallas import tpu as pltpu
from jax.sharding import PartitionSpec as P

HEAD_DIM = 128
QUERY_HEADS = 16
KV_HEADS = 4
GROUP = QUERY_HEADS // KV_HEADS
BLOCK_LEN = 128
BETA = 0.5
SCALING = 1.0 / math.sqrt(HEAD_DIM)
EXP2_SCALING = SCALING * math.log2(math.e)
CHUNK = 1024
EXTRA = 16
VMEM_LIMIT = 24 * 2**20
VMEM_ALL = 60 * 2**20
F32 = jnp.float32
BF16 = jnp.bfloat16


def dot(left, right, left_dim, right_dim):
    return lax.dot_general(
        left, right, (((left_dim,), (right_dim,)), ((), ())), preferred_element_type=F32
    )


def vmem():
    return pl.BlockSpec(memory_space=pltpu.VMEM)


def smem():
    return pl.BlockSpec(memory_space=pltpu.SMEM)


def whole(x):
    return pl.BlockSpec(x.shape, lambda i: (0,) * len(x.shape))


def params(limit=VMEM_LIMIT):
    return pltpu.CompilerParams(vmem_limit_bytes=limit)


def columns(seq, k, width, sharing=1):
    return pl.ds(pl.multiple_of((seq ^ k) // sharing * width, width), width)


def split_float(value):
    high = value.astype(BF16)
    rest = value - high.astype(F32)
    middle = rest.astype(BF16)
    low = (rest - middle.astype(F32)).astype(BF16)
    return high, middle, low


def join_float(rows, at):
    terms = [rows[at + i : at + i + 1, :].astype(F32) for i in range(3)]
    return terms[0] + terms[1] + terms[2]


def write_sums(target, sums, first_row):
    rows = [term.astype(F32) for value in sums for term in split_float(value)]
    rows += [jnp.zeros_like(rows[0])] * (EXTRA - len(rows))
    target[pl.ds(first_row, EXTRA), :] = jnp.concatenate(rows, axis=0).astype(BF16)


def farthest_first(blocks):
    blocks = list(blocks)
    return blocks[:1] + blocks[:0:-1]


def pack_prompt_body(lengths, keys, values, ratios, *blocks):
    seq = lax.axis_index("seq")
    rows = keys.shape[1]
    tokens = ratios.shape[2]
    width = 2 * HEAD_DIM
    sharing = len(blocks) // KV_HEADS
    positions = seq * tokens + lax.broadcasted_iota(jnp.int32, (1, tokens), 1)
    sums = []
    for slot in range(2):
        alive = positions < lengths[0, slot]
        total = jnp.sum(
            jnp.where(alive, ratios[0, slot : slot + 1, :], 0.0), axis=1, keepdims=True
        )
        sums.append(jnp.broadcast_to(total, (1, width)))
    for k, block in enumerate(blocks):
        head = columns(seq, k, HEAD_DIM, sharing)
        block[0:rows, 0:HEAD_DIM] = keys[0, :, head]
        block[0:rows, HEAD_DIM:width] = values[0, :, head]
        write_sums(block, sums, rows)


def pack_prompt(count, lengths, keys, values, ratios):
    shape = jax.ShapeDtypeStruct((keys.shape[1] + EXTRA, 2 * HEAD_DIM), BF16)
    return pl.pallas_call(
        pack_prompt_body,
        grid=(1,),
        out_shape=[shape] * count,
        in_specs=[smem(), whole(keys), whole(values), whole(ratios)],
        out_specs=[whole(shape)] * count,
        compiler_params=params(VMEM_ALL),
    )(lengths, keys, values, ratios)


def join_prompt_body(*refs):
    *blocks, joined_keys, joined_values = refs
    blocks = farthest_first(blocks)
    rows = blocks[0].shape[0] - EXTRA
    sums = [None, None]
    for k, block in enumerate(blocks):
        part = slice(k * rows, (k + 1) * rows)
        joined_keys[part, :] = block[0:rows, 0:HEAD_DIM]
        joined_values[part, :] = block[0:rows, HEAD_DIM:]
        extra = block[rows : rows + EXTRA, 0:HEAD_DIM]
        for slot in range(2):
            value = join_float(extra, 3 * slot)
            sums[slot] = value if sums[slot] is None else sums[slot] + value
    write_sums(joined_keys, sums, len(blocks) * rows)


def join_prompt(blocks):
    rows = len(blocks) * (blocks[0].shape[0] - EXTRA)
    return pl.pallas_call(
        join_prompt_body,
        out_shape=[
            jax.ShapeDtypeStruct((rows + EXTRA, HEAD_DIM), BF16),
            jax.ShapeDtypeStruct((rows, HEAD_DIM), BF16),
        ],
        in_specs=[vmem()] * len(blocks),
        out_specs=[vmem()] * 2,
        compiler_params=params(),
    )(*farthest_first(blocks))


def pack_slot_body(lengths, queries, grads, keys, values, *blocks):
    seq = lax.axis_index("seq")
    sharing = len(blocks) // KV_HEADS
    width = queries.shape[3] // len(blocks)
    at = 2 * width
    for k, block in enumerate(blocks):
        heads = columns(seq, k, width)
        block[:, 0:width] = queries[0, 0, :, heads]
        block[:, width:at] = grads[0, 0, :, heads]
        head = columns(seq, k, HEAD_DIM, sharing)
        block[:, at : at + HEAD_DIM] = keys[0, 0, :, head]
        block[:, at + HEAD_DIM :] = values[0, 0, :, head]


def pack_slot(slot, count, lengths, queries, grads, keys, values):
    tokens = queries.shape[2]
    wide = pl.BlockSpec((1, 1, tokens, queries.shape[3]), lambda i: (0, slot, 0, 0))
    narrow = pl.BlockSpec((1, 1, tokens, keys.shape[3]), lambda i: (0, slot, 0, 0))
    width = 2 * queries.shape[3] // count + 2 * HEAD_DIM
    block = pl.BlockSpec((tokens, width), lambda i: (0, 0))
    return pl.pallas_call(
        pack_slot_body,
        grid=(1,),
        out_shape=[jax.ShapeDtypeStruct((tokens, width), BF16)] * count,
        in_specs=[smem(), wide, wide, narrow, narrow],
        out_specs=[block] * count,
        compiler_params=params(VMEM_ALL),
    )(lengths, queries, grads, keys, values)


class Sizes:
    def __init__(self, count, prompt_rows, shard):
        self.count, self.prompt_rows, self.shard = count, prompt_rows, shard
        self.tokens = count * shard
        self.keys = prompt_rows + self.tokens
        self.heads = GROUP * KV_HEADS // count
        self.width = self.heads * HEAD_DIM
        self.tile_rows = self.heads * BLOCK_LEN
        self.tiles = self.tokens // BLOCK_LEN
        self.rows = self.heads * self.tokens

    def tile(self, number):
        return slice(number * self.tile_rows, (number + 1) * self.tile_rows)

    def spans(self, tile):
        end = self.prompt_rows + (tile + 1) * BLOCK_LEN
        cuts = list(range(0, self.prompt_rows, CHUNK))
        cuts += list(range(self.prompt_rows, end, CHUNK)) + [end]
        return [slice(a, b) for a, b in zip(cuts, cuts[1:])]

    def own_rows(self, seq, k):
        base = pl.multiple_of((seq ^ k) * self.shard, self.shard)
        places = []
        for u in range(self.shard // BLOCK_LEN):
            for g in range(self.heads):
                row = base * self.heads + (u * self.heads + g) * BLOCK_LEN
                rows = pl.ds(pl.multiple_of(row, BLOCK_LEN), BLOCK_LEN)
                places.append((slice(u * BLOCK_LEN, (u + 1) * BLOCK_LEN), g, rows))
        return base, places

    def resp_rows(self, base):
        return pl.ds(pl.multiple_of(self.prompt_rows + base, self.shard), self.shard)


def preference(slot, prefer, near, far):
    pair = lax.axis_index("pair")
    partner_index = pair ^ (lax.axis_size("pair") // 2)
    own_sign = jnp.where(prefer[pair] == 1, 1.0, -1.0)
    partner_sign = jnp.where(prefer[partner_index] == 1, 1.0, -1.0)
    own_margin = BETA * own_sign * (join_float(near, 0) - join_float(far, 3))
    partner_margin = BETA * partner_sign * (join_float(far, 0) - join_float(near, 3))
    if slot == 0:
        factor = -(BETA * own_sign / (1.0 + jnp.exp(own_margin)))
    else:
        factor = BETA * partner_sign / (1.0 + jnp.exp(partner_margin))
    loss = jnp.maximum(-own_margin, 0.0) + jnp.log1p(jnp.exp(-jnp.abs(own_margin)))
    return factor, loss


def load_tokens(sizes, length, factor, prompt, blocks, queries, grads, keys, values):
    seq = lax.axis_index("seq")
    prompt_rows, width = sizes.prompt_rows, sizes.width
    at = 2 * width
    keys[0:prompt_rows, :] = prompt[0][0:prompt_rows, :]
    if values is not None:
        values[0:prompt_rows, :] = prompt[1][...]
    for k, block in enumerate(blocks):
        base, places = sizes.own_rows(seq, k)
        positions = base + lax.broadcasted_iota(jnp.int32, (sizes.shard, HEAD_DIM), 0)
        scale = jnp.where(positions < length, factor, 0.0)
        for part, g, rows in places:
            head = g * HEAD_DIM
            queries[rows, :] = block[part, head : head + HEAD_DIM]
            grad = block[part, width + head : width + head + HEAD_DIM].astype(F32)
            grads[rows, :] = (scale[part] * grad).astype(BF16)
        rows = sizes.resp_rows(base)
        keys[rows, :] = block[:, at : at + HEAD_DIM]
        if values is not None:
            values[rows, :] = block[:, at + HEAD_DIM :]


def masked_scores(sizes, number, span, keys, queries):
    scores = dot(keys[span, :], queries, 1, 1) * EXP2_SCALING
    first = span.start - sizes.prompt_rows
    if span.stop - sizes.prompt_rows > number * BLOCK_LEN + 1:
        lane = lax.broadcasted_iota(jnp.int32, (1, sizes.tile_rows), 1)
        token = number * BLOCK_LEN + lane % BLOCK_LEN
        key = first + lax.broadcasted_iota(jnp.int32, (span.stop - span.start, 1), 0)
        scores = jnp.where(key <= token, scores, -jnp.inf)
    return scores


def softmax_terms(sizes, number, spans, keys, queries, scores, beside=lambda span: None):
    maxima = totals = None
    for span in spans:
        part = masked_scores(sizes, number, span, keys, queries)
        scores[span, :] = part
        top = jnp.max(part, axis=0, keepdims=True)
        maxima = top if maxima is None else jnp.maximum(maxima, top)
    for span in spans:
        part = jnp.exp2(scores[span, :] - maxima)
        beside(span)
        total = jnp.sum(part, axis=0, keepdims=True)
        totals = total if totals is None else totals + total
    return maxima + jnp.log2(totals)


def for_tiles(sizes, length, live, dead=None):
    for number in range(sizes.tiles):
        pl.when(number * BLOCK_LEN < length)(functools.partial(live, number))
        if dead is not None:
            pl.when(number * BLOCK_LEN >= length)(functools.partial(dead, number))


def first_body(slot, sizes, lengths, prefer, keys_in, sums, *refs):
    *blocks, prompt_dv, resp_dv, stats, q_all, c_all, k_all, scores, dv = refs
    length = lengths[0, slot]
    near, far = sums[sizes.prompt_rows :, :], keys_in[sizes.prompt_rows :, :]
    factor, _ = preference(slot, prefer, near, far)
    load_tokens(sizes, length, factor, (keys_in,), blocks, q_all, c_all, k_all, None)
    dv[...] = jnp.zeros_like(dv)

    def live(number):
        rows = sizes.tile(number)
        queries, grads = q_all[rows, :], c_all[rows, :]
        spans = sizes.spans(number)
        offset = softmax_terms(sizes, number, spans, k_all, queries, scores)
        stats[number, :, :] = offset
        for span in spans:
            weights = jnp.exp2(scores[span, :] - offset)
            dv[span, :] += dot(weights.astype(BF16), grads, 1, 0)

    for_tiles(sizes, length, live)
    prompt_dv[...] = dv[0 : sizes.prompt_rows, :].astype(prompt_dv.dtype)
    resp_dv[...] = dv[sizes.prompt_rows :, :]


def slot_body(slot, sizes, staged, lengths, prefer, keys_in, values_in, sums, *refs):
    count = sizes.count
    blocks, refs = refs[0:count], refs[count:]
    if staged:
        dv_in, stats, *refs = refs
    outs, refs = refs[0:count], refs[count:]
    if staged:
        prompt_dk, *scratch = refs
        q_all, c_all, k_all, v_all, scores, probs, dk, dq_all = scratch
    else:
        prompt_dk, prompt_dv, losses, *scratch = refs
        q_all, c_all, k_all, v_all, scores, probs, dk, dq_all, dv = scratch
    seq = lax.axis_index("seq")
    length = lengths[0, slot]
    prompt_rows, width = sizes.prompt_rows, sizes.width

    near, far = keys_in[prompt_rows:, :], sums[prompt_rows:, :]
    if slot == 1:
        near, far = far, near
    factor, loss = preference(slot, prefer, near, far)
    prompt = (keys_in, values_in)
    load_tokens(sizes, length, factor, prompt, blocks, q_all, c_all, k_all, v_all)
    dk[...] = jnp.zeros_like(dk)
    if not staged:
        losses[...] = loss
        dv[...] = jnp.zeros_like(dv)

    def live(number):
        rows = sizes.tile(number)
        queries, grads = q_all[rows, :], c_all[rows, :]
        spans = sizes.spans(number)

        def prob_grads(span):
            grad = dot(v_all[span, :], grads, 1, 1)
            probs[span, :] = grad
            return grad

        if staged:
            offset = stats[number, :, :]
        else:
            offset = softmax_terms(sizes, number, spans, k_all, queries, scores, prob_grads)
        inner = dq = None
        for span in spans:
            if staged:
                part = masked_scores(sizes, number, span, k_all, queries)
                part = jnp.exp2(part - offset)
                scores[span, :] = part
            else:
                part = jnp.exp2(scores[span, :] - offset)
            rounded = part.astype(BF16)
            grad = prob_grads(span) if staged else probs[span, :]
            part = jnp.sum(rounded.astype(F32) * grad, axis=0, keepdims=True)
            inner = part if inner is None else inner + part
            if not staged:
                dv[span, :] += dot(rounded, grads, 1, 0)
        for span in spans:
            part = scores[span, :] if staged else jnp.exp2(scores[span, :] - offset)
            part = (part * (probs[span, :] - inner)).astype(BF16)
            dk[span, :] += dot(part, queries, 1, 0)
            part = dot(k_all[span, :], part, 0, 0)
            dq = part if dq is None else dq + part
        dq_all[rows, :] = dq.T * SCALING

    def dead(number):
        dq_all[sizes.tile(number), :] = jnp.zeros((sizes.tile_rows, HEAD_DIM), F32)

    for_tiles(sizes, length, live, dead)

    for k, out in enumerate(outs):
        base, places = sizes.own_rows(seq, k)
        for part, g, rows in places:
            head = g * HEAD_DIM
            out[part, head : head + HEAD_DIM] = dq_all[rows, :].astype(out.dtype)
        rows = sizes.resp_rows(base)
        out[:, width : width + HEAD_DIM] = (dk[rows, :] * SCALING).astype(out.dtype)
        if staged:
            part = dv_in[pl.ds(base, sizes.shard), :]
        else:
            part = dv[rows, :]
        out[:, width + HEAD_DIM :] = part.astype(out.dtype)
    prompt_dk[...] = (dk[0:prompt_rows, :] * SCALING).astype(prompt_dk.dtype)
    if not staged:
        prompt_dv[...] = dv[0:prompt_rows, :]


def cost(flops):
    return pl.CostEstimate(flops=flops, bytes_accessed=2**20, transcendentals=0)


def slot_first(slot, lengths, prefer, keys, other, blocks):
    sizes = Sizes(len(blocks), keys.shape[0] - EXTRA, blocks[0].shape[0])
    out_shape = [
        jax.ShapeDtypeStruct((sizes.prompt_rows, HEAD_DIM), BF16),
        jax.ShapeDtypeStruct((sizes.tokens, HEAD_DIM), F32),
        jax.ShapeDtypeStruct((sizes.tiles, 1, sizes.tile_rows), F32),
    ]
    return pl.pallas_call(
        functools.partial(first_body, slot, sizes),
        out_shape=out_shape,
        in_specs=[smem(), smem()] + [vmem()] * (2 + sizes.count),
        out_specs=[vmem()] * len(out_shape),
        scratch_shapes=[
            pltpu.VMEM((sizes.rows, HEAD_DIM), BF16),
            pltpu.VMEM((sizes.rows, HEAD_DIM), BF16),
            pltpu.VMEM((sizes.keys, HEAD_DIM), BF16),
            pltpu.VMEM((sizes.keys, sizes.tile_rows), F32),
            pltpu.VMEM((sizes.keys, HEAD_DIM), F32),
        ],
        compiler_params=params(),
        cost_estimate=cost(4*10**9),
    )(lengths, prefer, keys, other, *blocks)


def slot_grads(slot, lengths, prefer, prompt, other, blocks, staged=()):
    keys, values = prompt
    sizes = Sizes(len(blocks), values.shape[0], blocks[0].shape[0])
    width = sizes.width + 2 * HEAD_DIM
    out_shape = [jax.ShapeDtypeStruct((sizes.shard, width), F32)]
    out_shape += [jax.ShapeDtypeStruct((sizes.shard, width), BF16)] * (sizes.count - 1)
    prompt_shape = (sizes.prompt_rows, HEAD_DIM)
    if staged:
        out_shape += [jax.ShapeDtypeStruct(prompt_shape, BF16)]
    else:
        out_shape += [jax.ShapeDtypeStruct(prompt_shape, F32)] * 2
        out_shape += [jax.ShapeDtypeStruct((1, HEAD_DIM), F32)]
    in_specs = [smem(), smem()] + [vmem()] * (3 + sizes.count + len(staged))
    scratch = [
        pltpu.VMEM((sizes.rows, HEAD_DIM), BF16),
        pltpu.VMEM((sizes.rows, HEAD_DIM), BF16),
        pltpu.VMEM((sizes.keys, HEAD_DIM), BF16),
        pltpu.VMEM((sizes.keys, HEAD_DIM), BF16),
        pltpu.VMEM((sizes.keys, sizes.tile_rows), F32),
        pltpu.VMEM((sizes.keys, sizes.tile_rows), F32),
        pltpu.VMEM((sizes.keys, HEAD_DIM), F32),
        pltpu.VMEM((sizes.rows, HEAD_DIM), F32),
    ]
    if not staged:
        scratch += [pltpu.VMEM((sizes.keys, HEAD_DIM), F32)]
    return pl.pallas_call(
        functools.partial(slot_body, slot, sizes, bool(staged)),
        out_shape=out_shape,
        in_specs=in_specs,
        out_specs=[vmem()] * len(out_shape),
        scratch_shapes=scratch,
        compiler_params=params(),
        cost_estimate=cost(4*10**9 if staged else 4*10**9),
    )(lengths, prefer, keys, values, other, *blocks, *staged)


def add_body(near_keys, near_values, far_keys, far_values, *outs):
    rows = outs[0].shape[0]
    for k, out in enumerate(outs):
        part = slice(k * rows, (k + 1) * rows)
        total = near_keys[part, :] + far_keys[part, :].astype(F32)
        out[:, 0:HEAD_DIM] = total.astype(out.dtype)
        total = near_values[part, :] + far_values[part, :].astype(F32)
        out[:, HEAD_DIM:] = total.astype(out.dtype)


def add_prompt(count, *terms):
    rows = terms[0].shape[0] // count
    out_shape = [jax.ShapeDtypeStruct((rows, 2 * HEAD_DIM), F32)]
    out_shape += [jax.ShapeDtypeStruct((rows, 2 * HEAD_DIM), BF16)] * (count - 1)
    return pl.pallas_call(
        add_body,
        out_shape=out_shape,
        in_specs=[vmem()] * 4,
        out_specs=[vmem()] * count,
        compiler_params=params(),
    )(*terms)


def head_sum(blocks, k, first):
    part = slice(first, first + HEAD_DIM)
    total = blocks[k][:, part].astype(F32)
    for i in range(1, len(blocks) // KV_HEADS):
        total = total + blocks[k + i][:, part].astype(F32)
    return total


def spread_slots_body(count, *refs):
    seq = lax.axis_index("seq")
    sharing = count // KV_HEADS
    resp_dq, resp_dk, resp_dv = refs[2 * count :]
    at = resp_dq.shape[3] // count
    for slot in range(2):
        blocks = farthest_first(refs[slot * count : (slot + 1) * count])
        for k, block in enumerate(blocks):
            resp_dq[0, slot, :, columns(seq, k, at)] = block[:, 0:at].astype(F32)
        for k in range(0, count, sharing):
            head = columns(seq, k, HEAD_DIM, sharing)
            resp_dk[0, slot, :, head] = head_sum(blocks, k, at)
            resp_dv[0, slot, :, head] = head_sum(blocks, k, at + HEAD_DIM)


def spread_slots(blocks_0, blocks_1):
    count = len(blocks_0)
    shard = blocks_0[0].shape[0]
    kv_width = KV_HEADS * HEAD_DIM
    out_shape = [jax.ShapeDtypeStruct((1, 2, shard, QUERY_HEADS * HEAD_DIM), F32)]
    out_shape += [jax.ShapeDtypeStruct((1, 2, shard, kv_width), F32)] * 2
    return pl.pallas_call(
        functools.partial(spread_slots_body, count),
        grid=(1,),
        out_shape=out_shape,
        in_specs=[whole(b) for b in (*blocks_0, *blocks_1)],
        out_specs=[whole(s) for s in out_shape],
        compiler_params=params(),
    )(*farthest_first(blocks_0), *farthest_first(blocks_1))


def spread_prompt_body(*refs):
    seq = lax.axis_index("seq")
    *blocks, prompt_dk, prompt_dv = refs
    blocks = farthest_first(blocks)
    sharing = len(blocks) // KV_HEADS
    for k in range(0, len(blocks), sharing):
        head = columns(seq, k, HEAD_DIM, sharing)
        prompt_dk[0, :, head] = head_sum(blocks, k, 0)
        prompt_dv[0, :, head] = head_sum(blocks, k, HEAD_DIM)


def spread_prompt(blocks):
    shape = jax.ShapeDtypeStruct((1, blocks[0].shape[0], KV_HEADS * HEAD_DIM), F32)
    return pl.pallas_call(
        spread_prompt_body,
        grid=(1,),
        out_shape=[shape] * 2,
        in_specs=[whole(b) for b in blocks],
        out_specs=[whole(shape)] * 2,
        compiler_params=params(),
    )(*farthest_first(blocks))


def exchange(blocks):
    count = len(blocks)
    received = {0: blocks[0]}
    for k in reversed(range(1, count)):
        received[k] = lax.ppermute(blocks[k], "seq", [(i, i ^ k) for i in range(count)])
    return [received[k] for k in range(count)]


def partner(x):
    count = lax.axis_size("pair")
    return lax.ppermute(x, "pair", [(i, i ^ count // 2) for i in range(count)])


def after(x, *earlier):
    return lax.optimization_barrier((x, earlier))[0]


def on_device(
    prompt_keys,
    prompt_values,
    resp_queries,
    resp_keys,
    resp_values,
    seq_grad,
    token_logratio,
    resp_len,
    prefer,
):
    count = lax.axis_size("seq")
    slot_args = (resp_queries, seq_grad, resp_keys, resp_values)
    packed = pack_prompt(count, resp_len, prompt_keys, prompt_values, token_logratio)
    prompt_blocks = exchange(packed)
    packed_1 = pack_slot(1, count, after(resp_len, packed), *slot_args)
    blocks_1 = exchange(packed_1)
    near_keys, near_values = join_prompt(after(prompt_blocks, packed_1[0]))
    far_keys = partner(near_keys)
    far_values = partner(near_values)
    packed_0 = pack_slot(0, count, after(resp_len, near_keys), *slot_args)
    blocks_0 = exchange(packed_0)
    lengths = after(resp_len, packed_0[0])
    share_values, *staged = slot_first(1, lengths, prefer, far_keys, near_keys, blocks_1)
    returned_values = partner(share_values)
    far = (far_keys, far_values)
    *outs_1, share_keys = slot_grads(1, lengths, prefer, far, near_keys, blocks_1, staged)
    returned_keys = partner(share_keys)
    outs_1 = exchange(outs_1)
    lengths = after(resp_len, share_keys)
    near = (near_keys, near_values)
    *outs_0, own_keys, own_values, losses = slot_grads(
        0, lengths, prefer, near, far_keys, blocks_0
    )
    outs_0 = exchange(outs_0)
    prompt_grads = exchange(
        add_prompt(count, own_keys, own_values, returned_keys, returned_values)
    )
    resp_grads = spread_slots(outs_0, outs_1)
    return (*spread_prompt(prompt_grads), *resp_grads, losses[0, 0:1])


def solution(mesh):
    in_specs = (
        P("pair", "seq", None),
        P("pair", "seq", None),
        P("pair", None, "seq", None),
        P("pair", None, "seq", None),
        P("pair", None, "seq", None),
        P("pair", None, "seq", None),
        P("pair", None, "seq"),
        P("pair", None),
        P(),
    )
    out_specs = (
        P("pair", "seq", None),
        P("pair", "seq", None),
        P("pair", None, "seq", None),
        P("pair", None, "seq", None),
        P("pair", None, "seq", None),
        P("pair"),
    )
    return jax.shard_map(
        on_device, mesh=mesh, in_specs=in_specs, out_specs=out_specs, check_vma=False
    )
```

```python
import functools
import math

import jax
import jax.numpy as jnp
from jax import lax
from jax.experimental import pallas as pl
from jax.experimental.pallas import tpu as pltpu
from jax.sharding import PartitionSpec as P

HEAD_DIM = 128
QUERY_HEADS = 16
KV_HEADS = 4
GROUP = QUERY_HEADS // KV_HEADS
BLOCK_LEN = 128
BETA = 0.5
SCALING = 1.0 / math.sqrt(HEAD_DIM)
EXP2_SCALING = SCALING * math.log2(math.e)
CHUNK = 1024
EXTRA = 16
VMEM_LIMIT = 24 * 2**20
VMEM_ALL = 60 * 2**20
F32 = jnp.float32
BF16 = jnp.bfloat16


def dot(left, right, left_dim, right_dim):
    return lax.dot_general(
        left, right, (((left_dim,), (right_dim,)), ((), ())), preferred_element_type=F32
    )


def vmem():
    return pl.BlockSpec(memory_space=pltpu.VMEM)


def smem():
    return pl.BlockSpec(memory_space=pltpu.SMEM)


def whole(x):
    return pl.BlockSpec(x.shape, lambda i: (0,) * len(x.shape))


def params(limit=VMEM_LIMIT):
    return pltpu.CompilerParams(vmem_limit_bytes=limit)


def columns(seq, k, width, sharing=1):
    return pl.ds(pl.multiple_of((seq ^ k) // sharing * width, width), width)


def split_float(value):
    high = value.astype(BF16)
    rest = value - high.astype(F32)
    middle = rest.astype(BF16)
    low = (rest - middle.astype(F32)).astype(BF16)
    return high, middle, low


def join_float(rows, at):
    terms = [rows[at + i : at + i + 1, :].astype(F32) for i in range(3)]
    return terms[0] + terms[1] + terms[2]


def write_sums(target, sums, first_row):
    rows = [term.astype(F32) for value in sums for term in split_float(value)]
    rows += [jnp.zeros_like(rows[0])] * (EXTRA - len(rows))
    target[pl.ds(first_row, EXTRA), :] = jnp.concatenate(rows, axis=0).astype(BF16)


def farthest_first(blocks):
    blocks = list(blocks)
    return blocks[:1] + blocks[:0:-1]


def pack_prompt_body(lengths, keys, values, ratios, *blocks):
    seq = lax.axis_index("seq")
    rows = keys.shape[1]
    tokens = ratios.shape[2]
    width = 2 * HEAD_DIM
    sharing = len(blocks) // KV_HEADS
    positions = seq * tokens + lax.broadcasted_iota(jnp.int32, (1, tokens), 1)
    sums = []
    for slot in range(2):
        alive = positions < lengths[0, slot]
        total = jnp.sum(
            jnp.where(alive, ratios[0, slot : slot + 1, :], 0.0), axis=1, keepdims=True
        )
        sums.append(jnp.broadcast_to(total, (1, width)))
    for k, block in enumerate(blocks):
        head = columns(seq, k, HEAD_DIM, sharing)
        block[0:rows, 0:HEAD_DIM] = keys[0, :, head]
        block[0:rows, HEAD_DIM:width] = values[0, :, head]
        write_sums(block, sums, rows)


def pack_prompt(count, lengths, keys, values, ratios):
    shape = jax.ShapeDtypeStruct((keys.shape[1] + EXTRA, 2 * HEAD_DIM), BF16)
    return pl.pallas_call(
        pack_prompt_body,
        grid=(1,),
        out_shape=[shape] * count,
        in_specs=[smem(), whole(keys), whole(values), whole(ratios)],
        out_specs=[whole(shape)] * count,
        compiler_params=params(VMEM_ALL),
    )(lengths, keys, values, ratios)


def join_prompt_body(*refs):
    *blocks, joined_keys, joined_values = refs
    blocks = farthest_first(blocks)
    rows = blocks[0].shape[0] - EXTRA
    sums = [None, None]
    for k, block in enumerate(blocks):
        part = slice(k * rows, (k + 1) * rows)
        joined_keys[part, :] = block[0:rows, 0:HEAD_DIM]
        joined_values[part, :] = block[0:rows, HEAD_DIM:]
        extra = block[rows : rows + EXTRA, 0:HEAD_DIM]
        for slot in range(2):
            value = join_float(extra, 3 * slot)
            sums[slot] = value if sums[slot] is None else sums[slot] + value
    write_sums(joined_keys, sums, len(blocks) * rows)


def join_prompt(blocks):
    rows = len(blocks) * (blocks[0].shape[0] - EXTRA)
    return pl.pallas_call(
        join_prompt_body,
        out_shape=[
            jax.ShapeDtypeStruct((rows + EXTRA, HEAD_DIM), BF16),
            jax.ShapeDtypeStruct((rows, HEAD_DIM), BF16),
        ],
        in_specs=[vmem()] * len(blocks),
        out_specs=[vmem()] * 2,
        compiler_params=params(),
    )(*farthest_first(blocks))


def pack_slot_body(lengths, queries, grads, keys, values, *blocks):
    seq = lax.axis_index("seq")
    sharing = len(blocks) // KV_HEADS
    width = queries.shape[3] // len(blocks)
    at = 2 * width
    for k, block in enumerate(blocks):
        heads = columns(seq, k, width)
        block[:, 0:width] = queries[0, 0, :, heads]
        block[:, width:at] = grads[0, 0, :, heads]
        head = columns(seq, k, HEAD_DIM, sharing)
        block[:, at : at + HEAD_DIM] = keys[0, 0, :, head]
        block[:, at + HEAD_DIM :] = values[0, 0, :, head]


def pack_slot(slot, count, lengths, queries, grads, keys, values):
    tokens = queries.shape[2]
    wide = pl.BlockSpec((1, 1, tokens, queries.shape[3]), lambda i: (0, slot, 0, 0))
    narrow = pl.BlockSpec((1, 1, tokens, keys.shape[3]), lambda i: (0, slot, 0, 0))
    width = 2 * queries.shape[3] // count + 2 * HEAD_DIM
    block = pl.BlockSpec((tokens, width), lambda i: (0, 0))
    return pl.pallas_call(
        pack_slot_body,
        grid=(1,),
        out_shape=[jax.ShapeDtypeStruct((tokens, width), BF16)] * count,
        in_specs=[smem(), wide, wide, narrow, narrow],
        out_specs=[block] * count,
        compiler_params=params(VMEM_ALL),
    )(lengths, queries, grads, keys, values)


class Sizes:
    def __init__(self, count, prompt_rows, shard):
        self.count, self.prompt_rows, self.shard = count, prompt_rows, shard
        self.tokens = count * shard
        self.keys = prompt_rows + self.tokens
        self.heads = GROUP * KV_HEADS // count
        self.width = self.heads * HEAD_DIM
        self.tile_rows = self.heads * BLOCK_LEN
        self.tiles = self.tokens // BLOCK_LEN
        self.rows = self.heads * self.tokens

    def tile(self, number):
        return slice(number * self.tile_rows, (number + 1) * self.tile_rows)

    def spans(self, tile):
        end = self.prompt_rows + (tile + 1) * BLOCK_LEN
        cuts = list(range(0, self.prompt_rows, CHUNK))
        cuts += list(range(self.prompt_rows, end, CHUNK)) + [end]
        return [slice(a, b) for a, b in zip(cuts, cuts[1:])]

    def own_rows(self, seq, k):
        base = pl.multiple_of((seq ^ k) * self.shard, self.shard)
        places = []
        for u in range(self.shard // BLOCK_LEN):
            for g in range(self.heads):
                row = base * self.heads + (u * self.heads + g) * BLOCK_LEN
                rows = pl.ds(pl.multiple_of(row, BLOCK_LEN), BLOCK_LEN)
                places.append((slice(u * BLOCK_LEN, (u + 1) * BLOCK_LEN), g, rows))
        return base, places

    def resp_rows(self, base):
        return pl.ds(pl.multiple_of(self.prompt_rows + base, self.shard), self.shard)


def preference(slot, prefer, near, far):
    pair = lax.axis_index("pair")
    partner_index = pair ^ (lax.axis_size("pair") // 2)
    own_sign = jnp.where(prefer[pair] == 1, 1.0, -1.0)
    partner_sign = jnp.where(prefer[partner_index] == 1, 1.0, -1.0)
    own_margin = BETA * own_sign * (join_float(near, 0) - join_float(far, 3))
    partner_margin = BETA * partner_sign * (join_float(far, 0) - join_float(near, 3))
    if slot == 0:
        factor = -(BETA * own_sign / (1.0 + jnp.exp(own_margin)))
    else:
        factor = BETA * partner_sign / (1.0 + jnp.exp(partner_margin))
    loss = jnp.maximum(-own_margin, 0.0) + jnp.log1p(jnp.exp(-jnp.abs(own_margin)))
    return factor, loss


def load_tokens(sizes, length, factor, prompt, blocks, queries, grads, keys, values):
    seq = lax.axis_index("seq")
    prompt_rows, width = sizes.prompt_rows, sizes.width
    at = 2 * width
    keys[0:prompt_rows, :] = prompt[0][0:prompt_rows, :]
    if values is not None:
        values[0:prompt_rows, :] = prompt[1][...]
    for k, block in enumerate(blocks):
        base, places = sizes.own_rows(seq, k)
        positions = base + lax.broadcasted_iota(jnp.int32, (sizes.shard, HEAD_DIM), 0)
        scale = jnp.where(positions < length, factor, 0.0)
        for part, g, rows in places:
            head = g * HEAD_DIM
            queries[rows, :] = block[part, head : head + HEAD_DIM]
            grad = block[part, width + head : width + head + HEAD_DIM].astype(F32)
            grads[rows, :] = (scale[part] * grad).astype(BF16)
        rows = sizes.resp_rows(base)
        keys[rows, :] = block[:, at : at + HEAD_DIM]
        if values is not None:
            values[rows, :] = block[:, at + HEAD_DIM :]


def masked_scores(sizes, number, span, keys, queries):
    scores = dot(keys[span, :], queries, 1, 1) * EXP2_SCALING
    first = span.start - sizes.prompt_rows
    if span.stop - sizes.prompt_rows > number * BLOCK_LEN + 1:
        lane = lax.broadcasted_iota(jnp.int32, (1, sizes.tile_rows), 1)
        token = number * BLOCK_LEN + lane % BLOCK_LEN
        key = first + lax.broadcasted_iota(jnp.int32, (span.stop - span.start, 1), 0)
        scores = jnp.where(key <= token, scores, -jnp.inf)
    return scores


def softmax_terms(sizes, number, spans, keys, queries, scores, beside=lambda span: None):
    maxima = totals = None
    for span in spans:
        part = masked_scores(sizes, number, span, keys, queries)
        scores[span, :] = part
        top = jnp.max(part, axis=0, keepdims=True)
        maxima = top if maxima is None else jnp.maximum(maxima, top)
    for span in spans:
        part = jnp.exp2(scores[span, :] - maxima)
        beside(span)
        total = jnp.sum(part, axis=0, keepdims=True)
        totals = total if totals is None else totals + total
    return maxima + jnp.log2(totals)


def for_tiles(sizes, length, live, dead=None):
    for number in range(sizes.tiles):
        pl.when(number * BLOCK_LEN < length)(functools.partial(live, number))
        if dead is not None:
            pl.when(number * BLOCK_LEN >= length)(functools.partial(dead, number))


def first_body(slot, sizes, lengths, prefer, keys_in, sums, *refs):
    *blocks, prompt_dv, resp_dv, stats, q_all, c_all, k_all, scores, tops, dv = refs
    length = lengths[0, slot]
    near, far = sums[sizes.prompt_rows :, :], keys_in[sizes.prompt_rows :, :]
    factor, _ = preference(slot, prefer, near, far)
    load_tokens(sizes, length, factor, (keys_in,), blocks, q_all, c_all, k_all, None)
    dv[...] = jnp.zeros_like(dv)

    def score_span(number, span):
        part = masked_scores(sizes, number, span, k_all, q_all[sizes.tile(number), :])
        scores[number % 2, span, :] = part
        return jnp.max(part, axis=0, keepdims=True)

    def keep_maxima(number, parts):
        tops[number % 2, :, :] = functools.reduce(jnp.maximum, parts)

    keep_maxima(0, [score_span(0, span) for span in sizes.spans(0)])

    def live(number):
        grads = c_all[sizes.tile(number), :]
        spans = sizes.spans(number)
        later = sizes.spans(number + 1) if number + 1 < sizes.tiles else []
        held, maxima = scores.at[number % 2], tops[number % 2, :, :]
        totals, next_tops = None, []
        for at, span in enumerate(spans):
            total = jnp.sum(jnp.exp2(held[span, :] - maxima), axis=0, keepdims=True)
            if at < len(later):
                next_tops.append(score_span(number + 1, later[at]))
            totals = total if totals is None else totals + total
        next_tops += [score_span(number + 1, span) for span in later[len(spans) :]]
        if later:
            keep_maxima(number + 1, next_tops)
        offset = maxima + jnp.log2(totals)
        stats[number, :, :] = offset
        for span in spans:
            weights = jnp.exp2(held[span, :] - offset)
            dv[span, :] += dot(weights.astype(BF16), grads, 1, 0)

    for_tiles(sizes, length, live)
    prompt_dv[...] = dv[0 : sizes.prompt_rows, :].astype(prompt_dv.dtype)
    resp_dv[...] = dv[sizes.prompt_rows :, :]


def slot_body(slot, sizes, staged, lengths, prefer, keys_in, values_in, sums, *refs):
    count = sizes.count
    blocks, refs = refs[0:count], refs[count:]
    if staged:
        dv_in, stats, *refs = refs
    outs, refs = refs[0:count], refs[count:]
    if staged:
        prompt_dk, *scratch = refs
        q_all, c_all, k_all, v_all, scores, probs, dk, dq_all = scratch
    else:
        prompt_dk, prompt_dv, losses, *scratch = refs
        q_all, c_all, k_all, v_all, scores, probs, dk, dq_all, dv = scratch
    seq = lax.axis_index("seq")
    length = lengths[0, slot]
    prompt_rows, width = sizes.prompt_rows, sizes.width

    near, far = keys_in[prompt_rows:, :], sums[prompt_rows:, :]
    if slot == 1:
        near, far = far, near
    factor, loss = preference(slot, prefer, near, far)
    prompt = (keys_in, values_in)
    load_tokens(sizes, length, factor, prompt, blocks, q_all, c_all, k_all, v_all)
    dk[...] = jnp.zeros_like(dk)
    if not staged:
        losses[...] = loss
        dv[...] = jnp.zeros_like(dv)

    def live(number):
        rows = sizes.tile(number)
        queries, grads = q_all[rows, :], c_all[rows, :]
        spans = sizes.spans(number)

        def prob_grads(span):
            grad = dot(v_all[span, :], grads, 1, 1)
            probs[span, :] = grad
            return grad

        if staged:
            offset = stats[number, :, :]
        else:
            offset = softmax_terms(sizes, number, spans, k_all, queries, scores, prob_grads)
        inner = dq = None
        for span in spans:
            if staged:
                part = masked_scores(sizes, number, span, k_all, queries)
                part = jnp.exp2(part - offset)
                scores[span, :] = part
            else:
                part = jnp.exp2(scores[span, :] - offset)
            rounded = part.astype(BF16)
            grad = prob_grads(span) if staged else probs[span, :]
            part = jnp.sum(rounded.astype(F32) * grad, axis=0, keepdims=True)
            inner = part if inner is None else inner + part
            if not staged:
                dv[span, :] += dot(rounded, grads, 1, 0)
        for span in spans:
            part = scores[span, :] if staged else jnp.exp2(scores[span, :] - offset)
            part = (part * (probs[span, :] - inner)).astype(BF16)
            dk[span, :] += dot(part, queries, 1, 0)
            part = dot(k_all[span, :], part, 0, 0)
            dq = part if dq is None else dq + part
        dq_all[rows, :] = dq.T * SCALING

    def dead(number):
        dq_all[sizes.tile(number), :] = jnp.zeros((sizes.tile_rows, HEAD_DIM), F32)

    for_tiles(sizes, length, live, dead)

    for k, out in enumerate(outs):
        base, places = sizes.own_rows(seq, k)
        for part, g, rows in places:
            head = g * HEAD_DIM
            out[part, head : head + HEAD_DIM] = dq_all[rows, :].astype(out.dtype)
        rows = sizes.resp_rows(base)
        out[:, width : width + HEAD_DIM] = (dk[rows, :] * SCALING).astype(out.dtype)
        if staged:
            part = dv_in[pl.ds(base, sizes.shard), :]
        else:
            part = dv[rows, :]
        out[:, width + HEAD_DIM :] = part.astype(out.dtype)
    prompt_dk[...] = (dk[0:prompt_rows, :] * SCALING).astype(prompt_dk.dtype)
    if not staged:
        prompt_dv[...] = dv[0:prompt_rows, :]


def cost(flops):
    return pl.CostEstimate(flops=flops, bytes_accessed=2**20, transcendentals=0)


def slot_first(slot, lengths, prefer, keys, other, blocks):
    sizes = Sizes(len(blocks), keys.shape[0] - EXTRA, blocks[0].shape[0])
    out_shape = [
        jax.ShapeDtypeStruct((sizes.prompt_rows, HEAD_DIM), BF16),
        jax.ShapeDtypeStruct((sizes.tokens, HEAD_DIM), F32),
        jax.ShapeDtypeStruct((sizes.tiles, 1, sizes.tile_rows), F32),
    ]
    return pl.pallas_call(
        functools.partial(first_body, slot, sizes),
        out_shape=out_shape,
        in_specs=[smem(), smem()] + [vmem()] * (2 + sizes.count),
        out_specs=[vmem()] * len(out_shape),
        scratch_shapes=[
            pltpu.VMEM((sizes.rows, HEAD_DIM), BF16),
            pltpu.VMEM((sizes.rows, HEAD_DIM), BF16),
            pltpu.VMEM((sizes.keys, HEAD_DIM), BF16),
            pltpu.VMEM((2, sizes.keys, sizes.tile_rows), F32),
            pltpu.VMEM((2, 1, sizes.tile_rows), F32),
            pltpu.VMEM((sizes.keys, HEAD_DIM), F32),
        ],
        compiler_params=params(),
        cost_estimate=cost(4*10**9),
    )(lengths, prefer, keys, other, *blocks)


def slot_grads(slot, lengths, prefer, prompt, other, blocks, staged=()):
    keys, values = prompt
    sizes = Sizes(len(blocks), values.shape[0], blocks[0].shape[0])
    width = sizes.width + 2 * HEAD_DIM
    out_shape = [jax.ShapeDtypeStruct((sizes.shard, width), F32)]
    out_shape += [jax.ShapeDtypeStruct((sizes.shard, width), BF16)] * (sizes.count - 1)
    prompt_shape = (sizes.prompt_rows, HEAD_DIM)
    if staged:
        out_shape += [jax.ShapeDtypeStruct(prompt_shape, BF16)]
    else:
        out_shape += [jax.ShapeDtypeStruct(prompt_shape, F32)] * 2
        out_shape += [jax.ShapeDtypeStruct((1, HEAD_DIM), F32)]
    in_specs = [smem(), smem()] + [vmem()] * (3 + sizes.count + len(staged))
    scratch = [
        pltpu.VMEM((sizes.rows, HEAD_DIM), BF16),
        pltpu.VMEM((sizes.rows, HEAD_DIM), BF16),
        pltpu.VMEM((sizes.keys, HEAD_DIM), BF16),
        pltpu.VMEM((sizes.keys, HEAD_DIM), BF16),
        pltpu.VMEM((sizes.keys, sizes.tile_rows), F32),
        pltpu.VMEM((sizes.keys, sizes.tile_rows), F32),
        pltpu.VMEM((sizes.keys, HEAD_DIM), F32),
        pltpu.VMEM((sizes.rows, HEAD_DIM), F32),
    ]
    if not staged:
        scratch += [pltpu.VMEM((sizes.keys, HEAD_DIM), F32)]
    return pl.pallas_call(
        functools.partial(slot_body, slot, sizes, bool(staged)),
        out_shape=out_shape,
        in_specs=in_specs,
        out_specs=[vmem()] * len(out_shape),
        scratch_shapes=scratch,
        compiler_params=params(),
        cost_estimate=cost(4*10**9 if staged else 4*10**9),
    )(lengths, prefer, keys, values, other, *blocks, *staged)


def add_body(near_keys, near_values, far_keys, far_values, *outs):
    rows = outs[0].shape[0]
    for k, out in enumerate(outs):
        part = slice(k * rows, (k + 1) * rows)
        total = near_keys[part, :] + far_keys[part, :].astype(F32)
        out[:, 0:HEAD_DIM] = total.astype(out.dtype)
        total = near_values[part, :] + far_values[part, :].astype(F32)
        out[:, HEAD_DIM:] = total.astype(out.dtype)


def add_prompt(count, *terms):
    rows = terms[0].shape[0] // count
    out_shape = [jax.ShapeDtypeStruct((rows, 2 * HEAD_DIM), F32)]
    out_shape += [jax.ShapeDtypeStruct((rows, 2 * HEAD_DIM), BF16)] * (count - 1)
    return pl.pallas_call(
        add_body,
        out_shape=out_shape,
        in_specs=[vmem()] * 4,
        out_specs=[vmem()] * count,
        compiler_params=params(),
    )(*terms)


def head_sum(blocks, k, first):
    part = slice(first, first + HEAD_DIM)
    total = blocks[k][:, part].astype(F32)
    for i in range(1, len(blocks) // KV_HEADS):
        total = total + blocks[k + i][:, part].astype(F32)
    return total


def spread_slots_body(count, *refs):
    seq = lax.axis_index("seq")
    sharing = count // KV_HEADS
    resp_dq, resp_dk, resp_dv = refs[2 * count :]
    at = resp_dq.shape[3] // count
    for slot in range(2):
        blocks = farthest_first(refs[slot * count : (slot + 1) * count])
        for k, block in enumerate(blocks):
            resp_dq[0, slot, :, columns(seq, k, at)] = block[:, 0:at].astype(F32)
        for k in range(0, count, sharing):
            head = columns(seq, k, HEAD_DIM, sharing)
            resp_dk[0, slot, :, head] = head_sum(blocks, k, at)
            resp_dv[0, slot, :, head] = head_sum(blocks, k, at + HEAD_DIM)


def spread_slots(blocks_0, blocks_1):
    count = len(blocks_0)
    shard = blocks_0[0].shape[0]
    kv_width = KV_HEADS * HEAD_DIM
    out_shape = [jax.ShapeDtypeStruct((1, 2, shard, QUERY_HEADS * HEAD_DIM), F32)]
    out_shape += [jax.ShapeDtypeStruct((1, 2, shard, kv_width), F32)] * 2
    return pl.pallas_call(
        functools.partial(spread_slots_body, count),
        grid=(1,),
        out_shape=out_shape,
        in_specs=[whole(b) for b in (*blocks_0, *blocks_1)],
        out_specs=[whole(s) for s in out_shape],
        compiler_params=params(),
    )(*farthest_first(blocks_0), *farthest_first(blocks_1))


def spread_prompt_body(*refs):
    seq = lax.axis_index("seq")
    *blocks, prompt_dk, prompt_dv = refs
    blocks = farthest_first(blocks)
    sharing = len(blocks) // KV_HEADS
    for k in range(0, len(blocks), sharing):
        head = columns(seq, k, HEAD_DIM, sharing)
        prompt_dk[0, :, head] = head_sum(blocks, k, 0)
        prompt_dv[0, :, head] = head_sum(blocks, k, HEAD_DIM)


def spread_prompt(blocks):
    shape = jax.ShapeDtypeStruct((1, blocks[0].shape[0], KV_HEADS * HEAD_DIM), F32)
    return pl.pallas_call(
        spread_prompt_body,
        grid=(1,),
        out_shape=[shape] * 2,
        in_specs=[whole(b) for b in blocks],
        out_specs=[whole(shape)] * 2,
        compiler_params=params(),
    )(*farthest_first(blocks))


def exchange(blocks):
    count = len(blocks)
    received = {0: blocks[0]}
    for k in reversed(range(1, count)):
        received[k] = lax.ppermute(blocks[k], "seq", [(i, i ^ k) for i in range(count)])
    return [received[k] for k in range(count)]


def partner(x):
    count = lax.axis_size("pair")
    return lax.ppermute(x, "pair", [(i, i ^ count // 2) for i in range(count)])


def after(x, *earlier):
    return lax.optimization_barrier((x, earlier))[0]


def on_device(
    prompt_keys,
    prompt_values,
    resp_queries,
    resp_keys,
    resp_values,
    seq_grad,
    token_logratio,
    resp_len,
    prefer,
):
    count = lax.axis_size("seq")
    slot_args = (resp_queries, seq_grad, resp_keys, resp_values)
    packed = pack_prompt(count, resp_len, prompt_keys, prompt_values, token_logratio)
    prompt_blocks = exchange(packed)
    packed_1 = pack_slot(1, count, after(resp_len, packed), *slot_args)
    blocks_1 = exchange(packed_1)
    near_keys, near_values = join_prompt(after(prompt_blocks, packed_1[0]))
    far_keys = partner(near_keys)
    far_values = partner(near_values)
    packed_0 = pack_slot(0, count, after(resp_len, near_keys), *slot_args)
    blocks_0 = exchange(packed_0)
    lengths = after(resp_len, packed_0[0])
    share_values, *staged = slot_first(1, lengths, prefer, far_keys, near_keys, blocks_1)
    returned_values = partner(share_values)
    far = (far_keys, far_values)
    *outs_1, share_keys = slot_grads(1, lengths, prefer, far, near_keys, blocks_1, staged)
    returned_keys = partner(share_keys)
    outs_1 = exchange(outs_1)
    lengths = after(resp_len, share_keys)
    near = (near_keys, near_values)
    *outs_0, own_keys, own_values, losses = slot_grads(
        0, lengths, prefer, near, far_keys, blocks_0
    )
    outs_0 = exchange(outs_0)
    prompt_grads = exchange(
        add_prompt(count, own_keys, own_values, returned_keys, returned_values)
    )
    resp_grads = spread_slots(outs_0, outs_1)
    return (*spread_prompt(prompt_grads), *resp_grads, losses[0, 0:1])


def solution(mesh):
    in_specs = (
        P("pair", "seq", None),
        P("pair", "seq", None),
        P("pair", None, "seq", None),
        P("pair", None, "seq", None),
        P("pair", None, "seq", None),
        P("pair", None, "seq", None),
        P("pair", None, "seq"),
        P("pair", None),
        P(),
    )
    out_specs = (
        P("pair", "seq", None),
        P("pair", "seq", None),
        P("pair", None, "seq", None),
        P("pair", None, "seq", None),
        P("pair", None, "seq", None),
        P("pair"),
    )
    return jax.shard_map(
        on_device, mesh=mesh, in_specs=in_specs, out_specs=out_specs, check_vma=False
    )
```
